128 devices in a mesh: lat: 8 (over z, core), lon: 16 (over y, x).
Axes of the slice: x: 4, y: 4, z: 4, core: 2. Of those that a mesh axis runs over, the one named last changes fastest.
Arguments:
- grid: bfloat16 [360, 1440, 256], P('lat', 'lon'), may hold values from -6 to 6
- dw_kernel: bfloat16 [1, 7, 7, 256], replicated, may hold values from -0.875 to 0.875
- norm_gain: float32 [1, 256], replicated, may hold values from 0.25 to 1.75
- w_up: bfloat16 [1, 256, 512], replicated, may hold values from -0.375 to 0.375
- w_down: bfloat16 [1, 512, 256], replicated, may hold values from -0.25 to 0.25
- w_read: bfloat16 [256, 64], replicated, may hold values from -0.375 to 0.375
- owner: int32 [1048576, 1], P(('lat', 'lon')), may hold values from 0 to 127; in each aligned block of 8192 rows (0 to 8191, 8192 to 16383, ...) at most 128 rows name the same one
- offsets: int32 [1048576], P(('lat', 'lon')), may hold values from 0 to 4049
- fractions: float32 [2, 1048576], P(None, ('lat', 'lon')), may hold values from 0 to 1
Outputs:
- readout: bfloat16 [1048576, 64], P(('lat', 'lon'))
The draws below stay inside these ranges and needn't reach their ends.
Inputs may be any that keep to these rules, and one draw needn't show every extreme that they name: `owner`: among the targets of one device (8192 rows in a row), no tile owns more than 128; some tile owns exactly 128.
All inputs are finite; a program needn't handle non-finite values.
Results may differ from the reference program's by a relative error of at most 0.0055.
Values may be sent and summed in bfloat16 or wider, within the bound.
A program may use at most 192 MiB of HBM per device.

```python
import math
import jax
import jax.numpy as jnp
import numpy as np
from jax import lax

CHANNELS = 256
HIDDEN_SIZE = 512
OUTC = 64
LAYERS = 1
TLAT = 45
TLON = 90
TGT_DEV = 8192
CAP = 128
NLAT = 360
NLON = 1440
TARGETS = 1048576
N_LAT = 8
N_LON = 16


def with_ends(values, own_key, least, largest):
    longest = values.shape.index(max(values.shape))
    spots = []
    for shift in (0, 1):
        where = [jax.random.randint(jax.random.fold_in(own_key, axis), (), 0, length) for axis, length in enumerate(values.shape)]
        where[longest] = (where[longest] + shift) % values.shape[longest]
        spots.append(tuple(where))
    return values.at[spots[0]].set(least).at[spots[1]].set(largest)


def block_levels(own_key, dims, split, smallest, largest):
    def one(dim, parts):
        steps = jax.random.uniform(jax.random.fold_in(jax.random.fold_in(own_key, 6), dim), (parts,), jnp.float32, smallest / len(split), largest / len(split))
        return jnp.repeat(jnp.exp(steps), dims[dim] // parts).reshape((-1,) + (1,) * (len(dims) - dim - 1))

    factor_of = one(*split[0])
    for cut in split[1:]:
        factor_of = factor_of * one(*cut)
    return factor_of


def shared_out(key, own, number, rows, count, top, bound, slope):
    ranking = jax.random.permutation(key, count)
    heavy_load, common = load_shares(count, rows * top, bound, slope, True), load_shares(count, rows * top, bound, slope, False)
    places = jnp.arange(count)

    def named(sizes, turn):
        used = int((sizes > 0).sum())
        fixed = max(1, used // 4)
        shifted = fixed + (places - fixed + turn * (used - fixed)) % max(1, count - fixed)
        return jnp.zeros((count,), jnp.int32).at[ranking[jnp.where(places < fixed, places, shifted)]].set(jnp.asarray(sizes, jnp.int32))

    sizes = jnp.where(number % 4 == 0, named(heavy_load, number // 4), named(common, number - number // 4 - 1))
    mixed = jax.random.permutation(jax.random.fold_in(own, 3), count)
    source_of, taker = mixed[0:count // 2 * 2:2], mixed[1:count // 2 * 2:2]
    room = jnp.minimum(sizes[source_of] - 1, bound - sizes[taker]) // 2
    room = jnp.where((source_of == ranking[0]) | (taker == ranking[0]) | (sizes[taker] == 0), 0, jnp.maximum(room, 0))
    shifted = jax.random.randint(jax.random.fold_in(own, 4), (count // 2,), 0, 1 << 20) % (room + 1)
    sizes = sizes.at[source_of].add(-shifted).at[taker].add(shifted)
    members = jnp.searchsorted(jnp.cumsum(sizes), jnp.arange(rows * top), side="right").astype(jnp.int32)
    table = members.reshape(top, rows).T
    table = table[jax.random.permutation(jax.random.fold_in(own, 1), rows)]
    turn = jax.random.randint(jax.random.fold_in(own, 2), (rows, 1), 0, top)
    return jnp.take_along_axis(table, (jnp.arange(top)[None, :] + turn) % top, axis=1)


def load_shares(count, total, limit, lean, full):
    loads = [(1 << 20) // math.isqrt(grade ** lean) + 1 for grade in range(1, count + 1)]
    largest = limit if full else min(limit, max(-(-total // count), total * loads[0] // sum(loads)))
    least = 1 if total - largest >= count - 1 else 0
    holding, surplus = [largest] + [least] * (count - 1), total - largest - least * (count - 1)
    while surplus > 0:
        movable = [i for i in range(1, count) if holding[i] < largest] or [i for i in range(1, count) if holding[i] < limit]
        pool, budget = sum([loads[i] for i in movable]), surplus
        for i in movable:
            more = min(limit - holding[i], max(1, budget * loads[i] // pool), surplus)
            holding[i] = holding[i] + more
            surplus = surplus - more
    return np.array(holding)


def bell_draw(key, extent, scale, reach, cuts=(), kind=jnp.bfloat16):
    values = jax.random.normal(key, extent, jnp.float32) * scale
    if len(cuts) > 0:
        values = block_levels(key, extent, cuts, -0.22, 0.18) * values
    return jnp.clip(values, min=-reach, max=reach).astype(kind)


def setup_inputs(seed: int = 0) -> dict:
    seeds = jax.random.split(jax.random.key(seed), 10)
    grid = bell_draw(seeds[0], (NLAT, NLON, CHANNELS), 1.0, 6.0, ((0, 8), (1, 16)))
    dw_kernel = bell_draw(seeds[1], (LAYERS, 7, 7, CHANNELS), 49 ** -0.5, 0.875)
    norm_gain = jnp.clip(1.0 + 0.15 * jax.random.normal(seeds[2], (LAYERS, CHANNELS), jnp.float32), 0.25, 1.75)
    w_up = bell_draw(seeds[3], (LAYERS, CHANNELS, HIDDEN_SIZE), CHANNELS ** -0.5, 0.375)
    w_down = bell_draw(seeds[4], (LAYERS, HIDDEN_SIZE, CHANNELS), HIDDEN_SIZE ** -0.5, 0.25)
    w_read = bell_draw(seeds[5], (CHANNELS, OUTC), CHANNELS ** -0.5, 0.375)
    owner_keys = jax.random.split(jax.random.fold_in(seeds[6], 1), TARGETS // TGT_DEV)
    owner_turns = jax.random.permutation(jax.random.fold_in(seeds[6], 3), TARGETS // TGT_DEV)
    owner = jax.vmap(lambda own, number: shared_out(jax.random.fold_in(seeds[6], 2), own, number, TGT_DEV, N_LAT * N_LON, 1, CAP, 2))(owner_keys, owner_turns).reshape((TARGETS, 1))
    offsets = with_ends(jax.random.randint(seeds[7], (TARGETS,), 0, TLAT * TLON), jax.random.fold_in(seeds[7], 1), 0, (TLAT * TLON) - 1).astype(jnp.int32)
    fractions = jnp.clip(1.0 * jax.random.uniform(seeds[8], (2, TARGETS), jnp.float32) ** block_levels(seeds[8], (2, TARGETS), ((1, 128),), -0.2, 0.2), 0.0, 1.0)
    return dict(grid=grid, dw_kernel=dw_kernel, norm_gain=norm_gain, w_up=w_up, w_down=w_down, w_read=w_read, owner=owner, offsets=offsets, fractions=fractions)


def conv_block(extended, kernel, gain, weight_up, weight_down):
    height = extended.shape[0] - 6
    breadth = extended.shape[1] - 6
    wide = extended.astype(jnp.float32)
    kernel_wide = kernel.astype(jnp.float32)
    summed = jnp.zeros((height, breadth, extended.shape[2]), jnp.float32)
    for shift_row in range(7):
        row_sum = wide[shift_row:shift_row + height, 0:breadth] * kernel_wide[shift_row, 0]
        for shift_col in range(1, 7):
            row_sum = row_sum + wide[shift_row:shift_row + height, shift_col:shift_col + breadth] * kernel_wide[shift_row, shift_col]
        summed = summed + row_sum
    centre_mean = lax.optimization_barrier(jnp.mean(summed, axis=-1, keepdims=True))
    centred = summed - centre_mean
    variance = lax.optimization_barrier(jnp.mean(centred * centred, axis=-1, keepdims=True))
    normed = (centred * lax.rsqrt(variance + 1e-06) * gain.astype(jnp.float32)).astype(jnp.bfloat16)
    flattened = normed.reshape(height * breadth, -1)
    hidden = jax.nn.gelu(jnp.dot(flattened, weight_up, preferred_element_type=jnp.float32)).astype(jnp.bfloat16)
    delta = jnp.dot(hidden, weight_down, preferred_element_type=jnp.float32)
    centre = wide[3:3 + height, 3:3 + breadth].reshape(height * breadth, -1)
    return (centre + delta).astype(jnp.bfloat16).reshape(height, breadth, -1)

def read_cells(table, stride, base_row, base_col, frac_y, frac_x):
    summed = jnp.zeros(base_row.shape + (table.shape[1],), jnp.float32)
    weight_total = jnp.zeros(base_row.shape, jnp.float32)
    for step_row in range(-1, 3):
        for step_col in range(-1, 3):
            position = (base_row + step_row + 2) * stride + base_col + step_col + 2
            weight = jnp.exp(-((frac_y - step_row) ** 2 + (frac_x - step_col) ** 2) * 0.5)
            summed = summed + weight[..., None] * table[position.astype(jnp.int32)].astype(jnp.float32)
            weight_total = weight_total + weight
    return (summed / weight_total[..., None]).astype(jnp.bfloat16)

def reference(grid, dw_kernel, norm_gain, w_up, w_down, w_read, owner, offsets, fractions):
    field = grid
    for layer in range(LAYERS):
        wrapped = jnp.concatenate([field[:, -3:], field, field[:, :3]], axis=1)
        padded = jnp.pad(wrapped, ((3, 3), (0, 0), (0, 0)))

        def band(index, padded=padded, layer=layer):
            piece = lax.dynamic_slice_in_dim(padded, index * TLAT, TLAT + 6, 0)
            return conv_block(piece, dw_kernel[layer], norm_gain[layer], w_up[layer], w_down[layer])
        field = lax.map(band, jnp.arange(N_LAT, dtype=jnp.int32)).reshape(NLAT, NLON, CHANNELS)
    projected = jnp.dot(field.reshape(-1, CHANNELS), w_read, preferred_element_type=jnp.float32).astype(jnp.bfloat16).reshape(NLAT, NLON, OUTC)
    wrapped = jnp.concatenate([projected[:, -2:], projected, projected[:, :2]], axis=1)
    table = jnp.pad(wrapped, ((2, 2), (0, 0), (0, 0))).reshape(-1, OUTC)
    tiles = owner[:, 0]
    base_row = tiles // N_LON * TLAT + offsets // TLON
    base_col = tiles % N_LON * TLON + offsets % TLON
    groups = N_LAT * N_LON

    def serve(packed):
        return read_cells(table, NLON + 4, packed[0], packed[1], packed[2], packed[3])
    result = lax.map(serve, (base_row.reshape(groups, -1), base_col.reshape(groups, -1), fractions[0].reshape(groups, -1), fractions[1].reshape(groups, -1)))
    return result.reshape(-1, OUTC)
```

```python
import functools
import jax, jax.numpy as jnp
from jax import lax
from jax.experimental import pallas as pl
from jax.experimental.pallas import tpu as pltpu
from jax.sharding import PartitionSpec as P
F32, BF16, I32 = jnp.float32, jnp.bfloat16, jnp.int32
VM = pltpu.VMEM


def route_kernel(owner_ref, off_ref, fr_ref, req_ref, row_ref, half_ref, hot_ref, val_ref):
    blocks = owner_ref.shape[0]
    sub = lax.broadcasted_iota(I32, (128, 128), 0)
    lane = lax.broadcasted_iota(I32, (128, 128), 1)
    upper = jnp.where(sub < lane, 1.0, 0.0).astype(BF16)
    prefix = jnp.concatenate([upper, jnp.ones((128, 128), BF16)], axis=1)
    group = 8

    def step(k, base):
        for u in range(group):
            b = k * group + u
            mine = owner_ref[pl.ds(b, 1), :]
            hot = jnp.where(mine == sub, 1.0, 0.0)
            hot16 = hot.astype(BF16)
            hot_ref[:, u * 128:(u + 1) * 128] = hot16
            sums = jnp.dot(hot16, prefix, preferred_element_type=F32)
            ranks = jnp.sum((sums[:, :128] + base) * hot, axis=0, keepdims=True)
            base = base + sums[:, 128:]
            rank = ranks.astype(I32)
            row_ref[pl.ds(b, 1), :] = mine * 64 + (rank & 63)
            half_ref[pl.ds(b, 1), :] = rank >> 6
            there = rank == sub
            off = off_ref[pl.ds(b, 1), :]
            fy = fr_ref[0:1, pl.ds(pl.multiple_of(b * 128, 128), 128)]
            fx = fr_ref[1:2, pl.ds(pl.multiple_of(b * 128, 128), 128)]
            fy_hi = fy.astype(BF16).astype(F32)
            fx_hi = fx.astype(BF16).astype(F32)
            parts = [(off >> 6).astype(F32), (off & 63).astype(F32), fy_hi, fy - fy_hi, fx_hi, fx - fx_hi]
            for p, part in enumerate(parts):
                val_ref[p * 128:(p + 1) * 128, u * 128:(u + 1) * 128] = jnp.where(there, part, 0.0).astype(BF16)
        acc = lax.dot_general(hot_ref[...], val_ref[...], (((1,), (1,)), ((), ())), preferred_element_type=F32)
        new = jnp.concatenate(
            [acc[:, 0:128] * 64.0 + acc[:, 128:256], acc[:, 256:384] + acc[:, 384:512], acc[:, 512:640] + acc[:, 640:768]],
            axis=1)
        req_ref[...] = jnp.where(k == 0, new, req_ref[...] + new)
        return base

    lax.fori_loop(0, blocks // group, step, jnp.zeros((128, 128), F32))


def route(owner, offsets, fractions):
    n = owner.shape[0]
    return pl.pallas_call(
        route_kernel,
        out_shape=[jax.ShapeDtypeStruct((128, 384), F32), jax.ShapeDtypeStruct((n // 128, 128), I32), jax.ShapeDtypeStruct((n // 128, 128), I32)],
        in_specs=[pl.BlockSpec(memory_space=VM)] * 3,
        out_specs=[pl.BlockSpec(memory_space=VM)] * 3,
        scratch_shapes=[VM((128, 1024), BF16), VM((768, 1024), BF16)],
        compiler_params=pltpu.CompilerParams(vmem_limit_bytes=32 << 20),
        name="route",
    )(owner.reshape(n // 128, 128), offsets.reshape(n // 128, 128), fractions)


def gather_kernel(idx_ref, fr_ref, table_ref, out_ref, g0_ref, g1_ref):
    lane = lax.broadcasted_iota(I32, (8, 128), 1)
    low = lane < 64
    one = jnp.where(low, -1.0, 0.0)
    two = jnp.where(low, 1.0, 2.0)
    one_c, two_c = -0.5 * one * one, -0.5 * two * two
    sources = out_ref.shape[0] // 64

    def fetch(d, g_ref):
        for s in range(128):
            at = pl.multiple_of(idx_ref[d, s], 8)
            g_ref[s * 8:(s + 1) * 8, :] = table_ref[pl.ds(at, 8), :]

    def work(d, g_ref):
        rows = fr_ref[pl.ds(d, 1), :]
        cy = jnp.transpose(jnp.broadcast_to(rows[:, 128:256], (128, 128)))
        cx = jnp.transpose(jnp.broadcast_to(rows[:, 256:384], (128, 128)))

        def part(g):
            fy = cy[g * 8:(g + 1) * 8, :]
            fx = cx[g * 8:(g + 1) * 8, :]
            am = jnp.exp(-fy - 0.5)
            a1 = jnp.exp(fy - 0.5)
            a2 = jnp.exp(fy + fy - 2.0)
            b0 = jnp.exp(fx * one + one_c)
            b1 = jnp.exp(fx * two + two_c)
            v = [g_ref[pl.ds(g * 64 + s, 8, stride=8), :] for s in range(8)]
            m = [v[2 * i] * b0 + v[2 * i + 1] * b1 for i in range(4)]
            tot = m[0] * am + m[1] + m[2] * a1 + m[3] * a2
            bs = b0 + b1
            bs = bs + pltpu.roll(bs, 64, 1)
            return tot / (bs * (am + 1.0 + a1 + a2))

        for g in range(0, 8, 2):
            res = []
            for q in (g, g + 1):
                p0, p1 = part(q), part(q + 8)
                res.append(jnp.where(low, p0, p1) + pltpu.roll(jnp.where(low, p1, p0), 64, 1))
            out_ref[pl.ds(pl.multiple_of(d * 64 + g * 8, 16), 16), :] = jnp.concatenate(res, axis=0).astype(BF16)

    fetch(0, g0_ref)

    def step(k, _):
        d = k * 2
        fetch(d + 1, g1_ref)
        work(d, g0_ref)
        fetch(jnp.minimum(d + 2, sources - 1), g0_ref)
        work(d + 1, g1_ref)
        return 0

    lax.fori_loop(0, sources // 2, step, 0)


def gather(idx, req, table):
    return pl.pallas_call(
        gather_kernel,
        out_shape=jax.ShapeDtypeStruct((128 * 64, 128), BF16),
        in_specs=[pl.BlockSpec(memory_space=pltpu.SMEM), pl.BlockSpec(memory_space=VM), pl.BlockSpec(memory_space=VM)],
        out_specs=pl.BlockSpec(memory_space=VM),
        scratch_shapes=[VM((1024, 128), F32), VM((1024, 128), F32)],
        compiler_params=pltpu.CompilerParams(vmem_limit_bytes=48 << 20),
        name="gather",
    )(idx, req, table)


def place_kernel(idx_ref, half_ref, ret_ref, out_ref, wide_ref, x0_ref, x1_ref):
    rows = ret_ref.shape[0]

    def widen(k, _):
        at = pl.multiple_of(k * 256, 256)
        wide_ref[pl.ds(at, 256), :] = ret_ref[pl.ds(at, 256), :].astype(F32)
        return 0

    lax.fori_loop(0, rows // 256, widen, 0)

    def fetch(k, x_ref):
        for t in range(128):
            x_ref[t:t + 1, :] = wide_ref[pl.ds(idx_ref[k, t], 1), :]

    def work(k, x_ref):
        y = jnp.transpose(x_ref[...])
        second = half_ref[pl.ds(k, 1), :] > 0
        out_ref[:, pl.ds(pl.multiple_of(k * 128, 128), 128)] = jnp.where(second, y[64:], y[:64]).astype(BF16)

    blocks = half_ref.shape[0]
    fetch(0, x0_ref)

    def step(j, _):
        k = j * 2
        fetch(k + 1, x1_ref)
        work(k, x0_ref)
        fetch(jnp.minimum(k + 2, blocks - 1), x0_ref)
        work(k + 1, x1_ref)
        return 0

    lax.fori_loop(0, blocks // 2, step, 0)


def place(idx, half, ret):
    n = half.shape[0] * 128
    return pl.pallas_call(
        place_kernel,
        out_shape=jax.ShapeDtypeStruct((64, n), BF16),
        in_specs=[pl.BlockSpec(memory_space=pltpu.SMEM), pl.BlockSpec(memory_space=VM), pl.BlockSpec(memory_space=VM)],
        out_specs=pl.BlockSpec(memory_space=VM),
        scratch_shapes=[VM(ret.shape, F32), VM((128, 128), F32), VM((128, 128), F32)],
        compiler_params=pltpu.CompilerParams(vmem_limit_bytes=32 << 20),
        name="place",
    )(idx, half, ret)


COLS, EXT = 96, 104


def grid_kernel(ext_ref, tap_ref, gain_ref, up_ref, down_ref, read_ref, out_ref, x_ref, tap8_ref, mix_ref, *, total_rows, tile_rows):
    first = lax.axis_index("lat") * tile_rows - 1
    for h in range(2):
        for t in range(49):
            tap8_ref[h, t * 8:(t + 1) * 8, :] = jnp.broadcast_to(tap_ref[t:t + 1, h * 128:(h + 1) * 128].astype(F32), (8, 128))

    def relay(r, _):
        for s in range(8):
            row = ext_ref[6 * s + r].astype(F32)
            for h in range(2):
                for c in range(EXT // 8):
                    x_ref[h, pl.ds((r * EXT + c * 8) * 8 + s, 8, stride=8), :] = row[c * 8:(c + 1) * 8, h * 128:(h + 1) * 128]
        return 0

    lax.fori_loop(0, 12, relay, 0)

    for h in range(2):
        def conv(c, _):
            acc = [None] * 6
            for b in range(7):
                x = [x_ref[h, pl.ds(pl.multiple_of((rr * EXT + c + b) * 8, 8), 8), :] for rr in range(12)]
                for a in range(7):
                    t = a * 7 + b
                    k = tap8_ref[h, t * 8:(t + 1) * 8, :]
                    for r in range(6):
                        p = x[r + a] * k
                        acc[r] = p if acc[r] is None else acc[r] + p
            for r in range(6):
                mix_ref[pl.ds(pl.multiple_of((r * COLS + c) * 8, 8), 8), h * 128:(h + 1) * 128] = acc[r]
            return 0

        lax.fori_loop(0, COLS, conv, 0)

    n = COLS * 8
    low = lax.broadcasted_iota(I32, (n, 128), 1) < 64
    strip = lax.broadcasted_iota(I32, (n, 128), 0) & 7

    def mlp(r, _):
        at = pl.multiple_of(r * n, n)
        m = mix_ref[pl.ds(at, n), :]
        m = m - jnp.mean(m, axis=1, keepdims=True)
        var = jnp.mean(m * m, axis=1, keepdims=True)
        normed = (m * lax.rsqrt(var + 1e-6) * gain_ref[...]).astype(BF16)
        hidden = jax.nn.gelu(jnp.dot(normed, up_ref[...], preferred_element_type=F32)).astype(BF16)
        delta = jnp.dot(hidden, down_ref[...], preferred_element_type=F32)
        mid = pl.multiple_of(((r + 3) * EXT + 3) * 8, 8)
        centre = jnp.concatenate([x_ref[0, pl.ds(mid, n), :], x_ref[1, pl.ds(mid, n), :]], axis=1)
        field = (centre + delta).astype(BF16)
        p = lax.dot_general(field, read_ref[...], (((1,), (1,)), ((), ())), preferred_element_type=F32)
        p = p.astype(BF16).astype(F32)
        row = first + strip * 6 + r
        p = jnp.where((row >= 0) & (row < total_rows), p, 0.0)
        out_ref[pl.ds(at, n), :] = jnp.where(low, p, jnp.concatenate([p[8:], p[:8]], axis=0))
        return 0

    lax.fori_loop(0, 6, mlp, 0)


def grid_block(ext, taps, gain, up, down, read2, total_rows, tile_rows):
    return pl.pallas_call(
        functools.partial(grid_kernel, total_rows=total_rows, tile_rows=tile_rows),
        out_shape=jax.ShapeDtypeStruct((6 * COLS * 8, 128), F32),
        in_specs=[pl.BlockSpec(memory_space=VM)] * 6,
        out_specs=pl.BlockSpec(memory_space=VM),
        scratch_shapes=[VM((2, 12 * EXT * 8, 128), F32), VM((2, 49 * 8, 128), F32), VM((6 * COLS * 8, 256), F32)],
        compiler_params=pltpu.CompilerParams(vmem_limit_bytes=48 << 20),
        name="grid_block",
    )(ext, taps, gain, up, down, read2)


def gather2_kernel(idx_ref, fr_ref, q_ref, out_ref, table_ref, g0_ref, g1_ref, *, tile_cols):
    def build(c, _):
        for r in range(6):
            for jj in range(2):
                q = q_ref[pl.ds(pl.multiple_of((r * COLS + c + 2 * jj) * 8, 8), 8), :]
                for i in range(4):
                    table_ref[pl.ds(((r - i + 3) * tile_cols + c) * 8 + 2 * i + jj, 8, stride=6 * tile_cols * 8), :] = q
        return 0

    lax.fori_loop(0, tile_cols, build, 0)
    gather_kernel(idx_ref, fr_ref, table_ref, out_ref, g0_ref, g1_ref)


def gather2(idx, req, q, tile_cols=90):
    return pl.pallas_call(
        functools.partial(gather2_kernel, tile_cols=tile_cols),
        out_shape=jax.ShapeDtypeStruct((128 * 64, 128), BF16),
        in_specs=[pl.BlockSpec(memory_space=pltpu.SMEM), pl.BlockSpec(memory_space=VM), pl.BlockSpec(memory_space=VM)],
        out_specs=pl.BlockSpec(memory_space=VM),
        scratch_shapes=[VM((51 * tile_cols * 8, 128), F32), VM((1024, 128), F32), VM((1024, 128), F32)],
        compiler_params=pltpu.CompilerParams(vmem_limit_bytes=48 << 20),
        name="gather",
    )(idx, req, q)


def shift(x, d_lat, d_lon):
    n_lat, n_lon = lax.axis_size("lat"), lax.axis_size("lon")
    pairs = []
    for p in range(n_lat):
        for q in range(n_lon):
            if 0 <= p + d_lat < n_lat:
                pairs.append((p * n_lon + q, (p + d_lat) * n_lon + (q + d_lon) % n_lon))
    return lax.ppermute(x, ("lat", "lon"), pairs)


def extended(grid):
    rows, cols = grid.shape[:2]
    top, bottom = grid[rows - 4:], grid[:5]
    parts = [
        [shift(top[:, cols - 4:], 1, 1), shift(top, 1, 0), shift(top[:, :5], 1, -1)],
        [shift(grid[:, cols - 4:], 0, 1), grid, shift(grid[:, :5], 0, -1)],
        [shift(bottom[:, cols - 4:], -1, 1), shift(bottom, -1, 0), shift(bottom[:, :5], -1, -1)],
    ]
    full = jnp.concatenate([jnp.concatenate(p, axis=1) for p in parts], axis=0)
    return jnp.pad(full, ((0, 0), (0, EXT - cols - 9), (0, 0)))


def shards(grid, dw_kernel, norm_gain, w_up, w_down, w_read, owner, offsets, fractions):
    tile_rows, tile_cols = grid.shape[:2]
    req, row, half = route(owner, offsets, fractions)
    ext = extended(grid)
    req = lax.all_to_all(req, ("lat", "lon"), split_axis=0, concat_axis=0, tiled=True)
    idx = (req[:, :128].astype(I32) + 3 * tile_cols) * 8
    read = w_read.T
    q = grid_block(
        ext, dw_kernel.reshape(49, -1), norm_gain, w_up[0], w_down[0], jnp.concatenate([read, read], axis=0),
        tile_rows * lax.axis_size("lat"), tile_rows)
    out = gather2(idx, req, q, tile_cols)
    ret = lax.all_to_all(out, ("lat", "lon"), split_axis=0, concat_axis=0, tiled=True)
    return place(row, half, ret).T


def solution(mesh):
    return jax.shard_map(
        shards,
        mesh=mesh,
        in_specs=(P("lat", "lon", None), P(), P(), P(), P(), P(), P(("lat", "lon"), None), P(("lat", "lon")), P(None, ("lat", "lon"))),
        out_specs=P(("lat", "lon"), None),
        check_vma=False,
    )
```

```python
import functools
import jax, jax.numpy as jnp
from jax import lax
from jax.experimental import pallas as pl
from jax.experimental.pallas import tpu as pltpu
from jax.sharding import PartitionSpec as P
F32, BF16, I32 = jnp.float32, jnp.bfloat16, jnp.int32
VM = pltpu.VMEM

COLS, EXT = 96, 104


def route_kernel(owner_ref, off_ref, fr_ref, req_ref, row_ref, half_ref, hot_ref, val_ref):
    blocks = owner_ref.shape[0]
    sub = lax.broadcasted_iota(I32, (128, 128), 0)
    lane = lax.broadcasted_iota(I32, (128, 128), 1)
    upper = jnp.where(sub < lane, 1.0, 0.0).astype(BF16)
    prefix = jnp.concatenate([upper, jnp.ones((128, 128), BF16)], axis=1)
    group = 8

    def step(k, base):
        for u in range(group):
            b = k * group + u
            mine = owner_ref[pl.ds(b, 1), :]
            hot = jnp.where(mine == sub, 1.0, 0.0)
            hot16 = hot.astype(BF16)
            hot_ref[:, u * 128:(u + 1) * 128] = hot16
            sums = jnp.dot(hot16, prefix, preferred_element_type=F32)
            ranks = jnp.sum((sums[:, :128] + base) * hot, axis=0, keepdims=True)
            base = base + sums[:, 128:]
            rank = ranks.astype(I32)
            row_ref[pl.ds(b, 1), :] = mine * 64 + (rank & 63)
            half_ref[pl.ds(b, 1), :] = rank >> 6
            there = rank == sub
            off = off_ref[pl.ds(b, 1), :]
            fy = fr_ref[0:1, pl.ds(pl.multiple_of(b * 128, 128), 128)]
            fx = fr_ref[1:2, pl.ds(pl.multiple_of(b * 128, 128), 128)]
            fy_hi = fy.astype(BF16).astype(F32)
            fx_hi = fx.astype(BF16).astype(F32)
            parts = [(off >> 6).astype(F32), (off & 63).astype(F32), fy_hi, fy - fy_hi, fx_hi, fx - fx_hi]
            for p, part in enumerate(parts):
                val_ref[p * 128:(p + 1) * 128, u * 128:(u + 1) * 128] = jnp.where(there, part, 0.0).astype(BF16)
        acc = lax.dot_general(hot_ref[...], val_ref[...], (((1,), (1,)), ((), ())), preferred_element_type=F32)
        new = jnp.concatenate(
            [acc[:, 0:128] * 64.0 + acc[:, 128:256], acc[:, 256:384] + acc[:, 384:512], acc[:, 512:640] + acc[:, 640:768]],
            axis=1)
        req_ref[...] = jnp.where(k == 0, new, req_ref[...] + new)
        return base

    lax.fori_loop(0, blocks // group, step, jnp.zeros((128, 128), F32))


def route(owner, offsets, fractions):
    n = owner.shape[0]
    return pl.pallas_call(
        route_kernel,
        out_shape=[jax.ShapeDtypeStruct((128, 384), F32), jax.ShapeDtypeStruct((n // 128, 128), I32), jax.ShapeDtypeStruct((n // 128, 128), I32)],
        in_specs=[pl.BlockSpec(memory_space=VM)] * 3,
        out_specs=[pl.BlockSpec(memory_space=VM)] * 3,
        scratch_shapes=[VM((128, 1024), BF16), VM((768, 1024), BF16)],
        compiler_params=pltpu.CompilerParams(vmem_limit_bytes=32 << 20),
        name="route",
    )(owner.reshape(n // 128, 128), offsets.reshape(n // 128, 128), fractions)


def grid_kernel(ext_ref, tap_ref, gain_ref, up_ref, down_ref, read_ref, out_ref, x_ref, tap8_ref, mix_ref, *, total_rows, tile_rows):
    first = lax.axis_index("lat") * tile_rows - 1
    for h in range(2):
        for t in range(49):
            tap8_ref[h, t * 8:(t + 1) * 8, :] = jnp.broadcast_to(tap_ref[t:t + 1, h * 128:(h + 1) * 128].astype(F32), (8, 128))

    def relay(r, _):
        for s in range(8):
            row = ext_ref[6 * s + r].astype(F32)
            for h in range(2):
                for c in range(EXT // 8):
                    x_ref[h, pl.ds((r * EXT + c * 8) * 8 + s, 8, stride=8), :] = row[c * 8:(c + 1) * 8, h * 128:(h + 1) * 128]
        return 0

    lax.fori_loop(0, 12, relay, 0)

    for h in range(2):
        def conv(c, _):
            acc = [None] * 6
            for b in range(7):
                x = [x_ref[h, pl.ds(pl.multiple_of((rr * EXT + c + b) * 8, 8), 8), :] for rr in range(12)]
                for a in range(7):
                    t = a * 7 + b
                    k = tap8_ref[h, t * 8:(t + 1) * 8, :]
                    for r in range(6):
                        p = x[r + a] * k
                        acc[r] = p if acc[r] is None else acc[r] + p
            for r in range(6):
                mix_ref[pl.ds(pl.multiple_of((r * COLS + c) * 8, 8), 8), h * 128:(h + 1) * 128] = acc[r]
            return 0

        lax.fori_loop(0, COLS, conv, 0)

    n = COLS * 8
    low = lax.broadcasted_iota(I32, (n, 128), 1) < 64
    strip = lax.broadcasted_iota(I32, (n, 128), 0) & 7

    def mlp(r, _):
        at = pl.multiple_of(r * n, n)
        m = mix_ref[pl.ds(at, n), :]
        m = m - jnp.mean(m, axis=1, keepdims=True)
        var = jnp.mean(m * m, axis=1, keepdims=True)
        normed = (m * lax.rsqrt(var + 1e-6) * gain_ref[...]).astype(BF16)
        hidden = jax.nn.gelu(jnp.dot(normed, up_ref[...], preferred_element_type=F32)).astype(BF16)
        delta = jnp.dot(hidden, down_ref[...], preferred_element_type=F32)
        mid = pl.multiple_of(((r + 3) * EXT + 3) * 8, 8)
        centre = jnp.concatenate([x_ref[0, pl.ds(mid, n), :], x_ref[1, pl.ds(mid, n), :]], axis=1)
        field = (centre + delta).astype(BF16)
        p = lax.dot_general(field, read_ref[...], (((1,), (1,)), ((), ())), preferred_element_type=F32)
        p = p.astype(BF16).astype(F32)
        row = first + strip * 6 + r
        p = jnp.where((row >= 0) & (row < total_rows), p, 0.0)
        out_ref[pl.ds(at, n), :] = jnp.where(low, p, jnp.concatenate([p[8:], p[:8]], axis=0))
        return 0

    lax.fori_loop(0, 6, mlp, 0)


def grid_block(ext, taps, gain, up, down, read2, total_rows, tile_rows):
    return pl.pallas_call(
        functools.partial(grid_kernel, total_rows=total_rows, tile_rows=tile_rows),
        out_shape=jax.ShapeDtypeStruct((6 * COLS * 8, 128), F32),
        in_specs=[pl.BlockSpec(memory_space=VM)] * 6,
        out_specs=pl.BlockSpec(memory_space=VM),
        scratch_shapes=[VM((2, 12 * EXT * 8, 128), F32), VM((2, 49 * 8, 128), F32), VM((6 * COLS * 8, 256), F32)],
        compiler_params=pltpu.CompilerParams(vmem_limit_bytes=48 << 20),
        name="grid_block",
    )(ext, taps, gain, up, down, read2)


def flat_weights(fr_ref, w_ref):
    fy, fx = fr_ref[:, 128:256], fr_ref[:, 256:384]
    a = [jnp.exp(-fy - 0.5), jnp.ones_like(fy), jnp.exp(fy - 0.5), jnp.exp(fy + fy - 2.0)]
    b = [jnp.exp(-fx - 0.5), jnp.ones_like(fx), jnp.exp(fx - 0.5), jnp.exp(fx + fx - 2.0)]
    scale = 1.0 / ((a[0] + a[1] + a[2] + a[3]) * (b[0] + b[1] + b[2] + b[3]))
    a = [x * scale for x in a]
    row = lax.broadcasted_iota(I32, (128, 1024), 0)
    col = lax.broadcasted_iota(I32, (128, 1024), 1)
    for s in range(8):
        one = jnp.where(col == row * 8 + s, 1.0, 0.0).astype(BF16)
        for half in range(2):
            plane = (a[s // 2] * b[2 * (s % 2) + half]).astype(BF16)
            part = jnp.dot(plane, one, preferred_element_type=F32)
            w_ref[half] = part if s == 0 else w_ref[half] + part


def build_table(q_ref, table_ref, tile_rows, tile_cols):
    sub = lax.broadcasted_iota(I32, (8, 128), 0)
    masks = {n: (sub & n) == 0 for n in (1, 2, 4)}

    def build(c, _):
        q = [[None] * 2 for _ in range(9)]
        for jj in range(2):
            for r in range(6):
                q[r][jj] = q_ref[pl.ds(pl.multiple_of((r * COLS + c + 2 * jj) * 8, 8), 8), :]
            for r in range(3):
                q[r + 6][jj] = pltpu.roll(q[r][jj], 7, 0)
        for r in range(6):
            v = [q[r + i][jj] for i in range(4) for jj in range(2)]
            for n in (4, 2, 1):
                new = list(v)
                for k in range(8):
                    if not k & n:
                        new[k] = jnp.where(masks[n], v[k], pltpu.roll(v[k + n], n, 0))
                        new[k + n] = jnp.where(masks[n], pltpu.roll(v[k], 8 - n, 0), v[k + n])
                v = new
            for k in range(8):
                if 6 * k + r < tile_rows:
                    table_ref[(6 * k + r) * tile_cols + c] = v[k]
        return 0

    lax.fori_loop(0, tile_cols, build, 0)


def read_source(idx_ref, d, table_ref, w_ref, out_ref, low):
    own = (lax.broadcasted_iota(I32, (32, 256), 1) >> 3) == lax.broadcasted_iota(I32, (32, 256), 0)
    sums = []
    for g in range(4):
        patches = []
        for s in range(32):
            patches.append(table_ref[idx_ref[d, g * 32 + s]])
        weights = [jnp.where(own, w_ref[h, pl.ds(d, 1), g * 256:(g + 1) * 256], 0.0) for h in range(2)]
        sums.append(jnp.dot(
            jnp.concatenate(weights, axis=0).astype(BF16), jnp.concatenate(patches, axis=0).astype(BF16),
            preferred_element_type=F32))
    for g in range(2):
        first, second = sums[g], sums[g + 2]
        keep = jnp.where(low, first[:32], second[32:])
        move = jnp.where(low, second[:32], first[32:])
        at = pl.multiple_of(d * 64 + g * 32, 32)
        out_ref[pl.ds(at, 32), :] = (keep + pltpu.roll(move, 64, 1)).astype(BF16)


def serve_kernel(idx_ref, fr_ref, q_ref, ret_ref, table_ref, w_ref, out_ref, send_sem, recv_sem, own_sem, *, tile_rows, tile_cols, n_lon, sources, unroll, turn):
    low = lax.broadcasted_iota(I32, (32, 128), 1) < 64
    flat_weights(fr_ref, w_ref)
    build_table(q_ref, table_ref, tile_rows, tile_cols)
    me = lax.axis_index("lat") * n_lon + lax.axis_index("lon")

    def rows(d):
        return pl.ds(pl.multiple_of(d * 64, 64), 64)

    def send(d):
        pltpu.make_async_remote_copy(
            src_ref=out_ref.at[rows(d)], dst_ref=ret_ref.at[rows(me)], send_sem=send_sem, recv_sem=recv_sem,
            device_id=(d // n_lon, d % n_lon), device_id_type=pl.DeviceIdType.MESH).start()

    own = pltpu.make_async_copy(out_ref.at[rows(me)], ret_ref.at[rows(me)], own_sem)

    def step(j, _):
        for u in range(unroll):
            d = (me + (j * unroll + u) * turn) % sources
            read_source(idx_ref, d, table_ref, w_ref, out_ref, low)
            if u:
                send(d)
            else:
                pl.when(j > 0)(functools.partial(send, d))
                pl.when(j == 0)(own.start)
        return 0

    lax.fori_loop(0, sources // unroll, step, 0)
    own.wait()
    most = pl.ds(0, (sources - 1) * 64)
    pltpu.make_async_copy(out_ref.at[most], ret_ref.at[most], send_sem).wait()
    pltpu.make_async_copy(out_ref.at[most], ret_ref.at[most], recv_sem).wait()


def serve(idx, req, q, tile_rows, tile_cols, n_lon):
    sources = idx.shape[0]
    return pl.pallas_call(
        functools.partial(serve_kernel, tile_rows=tile_rows, tile_cols=tile_cols, n_lon=n_lon, sources=sources, unroll=8, turn=37),
        out_shape=jax.ShapeDtypeStruct((sources * 64, 128), BF16),
        in_specs=[pl.BlockSpec(memory_space=pltpu.SMEM), pl.BlockSpec(memory_space=VM), pl.BlockSpec(memory_space=VM)],
        out_specs=pl.BlockSpec(memory_space=pl.ANY),
        scratch_shapes=[
            VM((tile_rows * tile_cols, 8, 128), F32), VM((2, 128, 1024), F32), VM((sources * 64, 128), BF16),
            pltpu.SemaphoreType.DMA, pltpu.SemaphoreType.DMA, pltpu.SemaphoreType.DMA],
        compiler_params=pltpu.CompilerParams(vmem_limit_bytes=48 << 20, has_side_effects=True),
        name="serve",
    )(idx, req, q)


def place_kernel(idx_ref, half_ref, ret_ref, out_ref, wide_ref, x0_ref, x1_ref):
    rows = ret_ref.shape[0]

    def widen(k, _):
        at = pl.multiple_of(k * 256, 256)
        wide_ref[pl.ds(at, 256), :] = ret_ref[pl.ds(at, 256), :].astype(F32)
        return 0

    lax.fori_loop(0, rows // 256, widen, 0)

    def fetch(k, x_ref):
        for t in range(128):
            x_ref[t:t + 1, :] = wide_ref[pl.ds(idx_ref[k, t], 1), :]

    def work(k, x_ref):
        y = jnp.transpose(x_ref[...])
        second = half_ref[pl.ds(k, 1), :] > 0
        out_ref[:, pl.ds(pl.multiple_of(k * 128, 128), 128)] = jnp.where(second, y[64:], y[:64]).astype(BF16)

    blocks = half_ref.shape[0]
    fetch(0, x0_ref)

    def step(j, _):
        k = j * 2
        fetch(k + 1, x1_ref)
        work(k, x0_ref)
        fetch(jnp.minimum(k + 2, blocks - 1), x0_ref)
        work(k + 1, x1_ref)
        return 0

    lax.fori_loop(0, blocks // 2, step, 0)


def place(idx, half, ret):
    n = half.shape[0] * 128
    return pl.pallas_call(
        place_kernel,
        out_shape=jax.ShapeDtypeStruct((64, n), BF16),
        in_specs=[pl.BlockSpec(memory_space=pltpu.SMEM), pl.BlockSpec(memory_space=VM), pl.BlockSpec(memory_space=VM)],
        out_specs=pl.BlockSpec(memory_space=VM),
        scratch_shapes=[VM(ret.shape, F32), VM((128, 128), F32), VM((128, 128), F32)],
        compiler_params=pltpu.CompilerParams(vmem_limit_bytes=32 << 20),
        name="place",
    )(idx, half, ret)


def shift(x, d_lat, d_lon):
    n_lat, n_lon = lax.axis_size("lat"), lax.axis_size("lon")
    pairs = []
    for p in range(n_lat):
        for q in range(n_lon):
            if 0 <= p + d_lat < n_lat:
                pairs.append((p * n_lon + q, (p + d_lat) * n_lon + (q + d_lon) % n_lon))
    return lax.ppermute(x, ("lat", "lon"), pairs)


def extended(grid):
    rows, cols = grid.shape[:2]
    top, bottom = grid[rows - 4:], grid[:5]
    parts = [
        [shift(top[:, cols - 4:], 1, 1), shift(top, 1, 0), shift(top[:, :5], 1, -1)],
        [shift(grid[:, cols - 4:], 0, 1), grid, shift(grid[:, :5], 0, -1)],
        [shift(bottom[:, cols - 4:], -1, 1), shift(bottom, -1, 0), shift(bottom[:, :5], -1, -1)],
    ]
    full = jnp.concatenate([jnp.concatenate(p, axis=1) for p in parts], axis=0)
    return jnp.pad(full, ((0, 0), (0, EXT - cols - 9), (0, 0)))


def shards(grid, dw_kernel, norm_gain, w_up, w_down, w_read, owner, offsets, fractions):
    tile_rows, tile_cols = grid.shape[:2]
    req, row, half = route(owner, offsets, fractions)
    ext = extended(grid)
    req = lax.all_to_all(req, ("lat", "lon"), split_axis=0, concat_axis=0, tiled=True)
    idx = req[:, :128].astype(I32)
    read = w_read.T
    q = grid_block(
        ext, dw_kernel.reshape(49, -1), norm_gain, w_up[0], w_down[0], jnp.concatenate([read, read], axis=0),
        tile_rows * lax.axis_size("lat"), tile_rows)
    ret = serve(idx, req, q, tile_rows, tile_cols, lax.axis_size("lon"))
    return place(row, half, ret).T


def solution(mesh):
    return jax.shard_map(
        shards,
        mesh=mesh,
        in_specs=(P("lat", "lon", None), P(), P(), P(), P(), P(), P(("lat", "lon"), None), P(("lat", "lon")), P(None, ("lat", "lon"))),
        out_specs=P(("lat", "lon"), None),
        check_vma=False,
    )
```

```python
import functools
import jax, jax.numpy as jnp
from jax import lax
from jax.experimental import pallas as pl
from jax.experimental.pallas import tpu as pltpu
from jax.sharding import PartitionSpec as P
F32, BF16, I32 = jnp.float32, jnp.bfloat16, jnp.int32
VM = pltpu.VMEM

COLS, EXT = 96, 112


def route_body(owner_ref, off_ref, fr_ref, req_ref, row_ref, half_ref, hot_ref, val_ref):
    blocks = owner_ref.shape[0]
    sub = lax.broadcasted_iota(I32, (128, 128), 0)
    lane = lax.broadcasted_iota(I32, (128, 128), 1)
    upper = jnp.where(sub < lane, 1.0, 0.0).astype(BF16)
    prefix = jnp.concatenate([upper, jnp.ones((128, 128), BF16)], axis=1)
    group = 8

    def step(k, base):
        for u in range(group):
            b = k * group + u
            mine = owner_ref[pl.ds(b, 1), :]
            hot = jnp.where(mine == sub, 1.0, 0.0)
            hot16 = hot.astype(BF16)
            hot_ref[:, u * 128:(u + 1) * 128] = hot16
            sums = jnp.dot(hot16, prefix, preferred_element_type=F32)
            ranks = jnp.sum((sums[:, :128] + base) * hot, axis=0, keepdims=True)
            base = base + sums[:, 128:]
            rank = ranks.astype(I32)
            row_ref[pl.ds(b, 1), :] = jnp.clip(mine, 0, 127) * 64 + (rank & 63)
            half_ref[pl.ds(b, 1), :] = rank >> 6
            there = rank == sub
            off = off_ref[pl.ds(b, 1), :]
            fy = fr_ref[0:1, pl.ds(pl.multiple_of(b * 128, 128), 128)]
            fx = fr_ref[1:2, pl.ds(pl.multiple_of(b * 128, 128), 128)]
            fy_hi = fy.astype(BF16).astype(F32)
            fx_hi = fx.astype(BF16).astype(F32)
            parts = [(off >> 6).astype(F32), (off & 63).astype(F32), fy_hi, fy - fy_hi, fx_hi, fx - fx_hi]
            for p, part in enumerate(parts):
                val_ref[p * 128:(p + 1) * 128, u * 128:(u + 1) * 128] = jnp.where(there, part, 0.0).astype(BF16)
        acc = lax.dot_general(hot_ref[...], val_ref[...], (((1,), (1,)), ((), ())), preferred_element_type=F32)
        new = [acc[:, 0:128] * 64.0 + acc[:, 128:256], acc[:, 256:384] + acc[:, 384:512], acc[:, 512:640] + acc[:, 640:768]]
        for q in range(3):
            at = pl.ds(q, 128, stride=8)
            req_ref[at, :] = jnp.where(k == 0, new[q], req_ref[at, :] + new[q])
        return base

    lax.fori_loop(0, blocks // group, step, jnp.zeros((128, 128), F32))


def grid_body(x_ref, tap8_ref, mix_ref, gain_ref, up_ref, down_ref, read_ref, q_ref, first, total_rows):
    for h in range(2):
        def conv(c, _):
            acc = [None] * 6
            for b in range(7):
                x = [x_ref[h, pl.ds(pl.multiple_of((rr * EXT + c + 4 + b) * 8, 8), 8), :] for rr in range(12)]
                for a in range(7):
                    t = a * 7 + b
                    k = tap8_ref[h, t * 8:(t + 1) * 8, :]
                    for r in range(6):
                        p = x[r + a] * k
                        acc[r] = p if acc[r] is None else acc[r] + p
            for r in range(6):
                mix_ref[pl.ds(pl.multiple_of((r * COLS + c) * 8, 8), 8), h * 128:(h + 1) * 128] = acc[r]
            return 0

        lax.fori_loop(0, COLS, conv, 0)

    n = COLS * 8
    low = lax.broadcasted_iota(I32, (n, 128), 1) < 64
    strip = lax.broadcasted_iota(I32, (n, 128), 0) & 7

    def mlp(r, _):
        at = pl.multiple_of(r * n, n)
        m = mix_ref[pl.ds(at, n), :]
        m = m - jnp.mean(m, axis=1, keepdims=True)
        var = jnp.mean(m * m, axis=1, keepdims=True)
        normed = (m * lax.rsqrt(var + 1e-6) * gain_ref[...]).astype(BF16)
        hidden = jax.nn.gelu(jnp.dot(normed, up_ref[...], preferred_element_type=F32)).astype(BF16)
        delta = jnp.dot(hidden, down_ref[...], preferred_element_type=F32)
        mid = pl.multiple_of(((r + 3) * EXT + 7) * 8, 8)
        centre = jnp.concatenate([x_ref[0, pl.ds(mid, n), :], x_ref[1, pl.ds(mid, n), :]], axis=1)
        field = (centre + delta).astype(BF16)
        p = lax.dot_general(field, read_ref[...], (((1,), (1,)), ((), ())), preferred_element_type=F32)
        p = p.astype(BF16).astype(F32)
        row = first + strip * 6 + r
        p = jnp.where((row >= 0) & (row < total_rows), p, 0.0)
        q_ref[pl.ds(at, n), :] = jnp.where(low, p, jnp.concatenate([p[8:], p[:8]], axis=0))
        return 0

    lax.fori_loop(0, 6, mlp, 0)


def flat_weights(fr_ref, w_ref):
    fy, fx = fr_ref[0], fr_ref[1]
    a = [jnp.exp(-fy - 0.5), jnp.ones_like(fy), jnp.exp(fy - 0.5), jnp.exp(fy + fy - 2.0)]
    b = [jnp.exp(-fx - 0.5), jnp.ones_like(fx), jnp.exp(fx - 0.5), jnp.exp(fx + fx - 2.0)]
    scale = 1.0 / ((a[0] + a[1] + a[2] + a[3]) * (b[0] + b[1] + b[2] + b[3]))
    a = [x * scale for x in a]
    row = lax.broadcasted_iota(I32, (128, 1024), 0)
    col = lax.broadcasted_iota(I32, (128, 1024), 1)
    for s in range(8):
        one = jnp.where(col == row * 8 + s, 1.0, 0.0).astype(BF16)
        for half in range(2):
            plane = (a[s // 2] * b[2 * (s % 2) + half]).astype(BF16)
            part = jnp.dot(plane, one, preferred_element_type=F32)
            w_ref[half] = part if s == 0 else w_ref[half] + part


def build_table(q_ref, table_ref, tile_rows, tile_cols):
    sub = lax.broadcasted_iota(I32, (8, 128), 0)
    masks = {n: (sub & n) == 0 for n in (1, 2, 4)}

    def build(c, _):
        q = [[None] * 2 for _ in range(9)]
        for jj in range(2):
            for r in range(6):
                q[r][jj] = q_ref[pl.ds(pl.multiple_of((r * COLS + c + 2 * jj) * 8, 8), 8), :]
            for r in range(3):
                q[r + 6][jj] = pltpu.roll(q[r][jj], 7, 0)
        for r in range(6):
            v = [q[r + i][jj] for i in range(4) for jj in range(2)]
            for n in (4, 2, 1):
                new = list(v)
                for k in range(8):
                    if not k & n:
                        new[k] = jnp.where(masks[n], v[k], pltpu.roll(v[k + n], n, 0))
                        new[k + n] = jnp.where(masks[n], pltpu.roll(v[k], 8 - n, 0), v[k + n])
                v = new
            for k in range(8):
                if 6 * k + r < tile_rows:
                    table_ref[(6 * k + r) * tile_cols + c] = v[k]
        return 0

    lax.fori_loop(0, tile_cols, build, 0)


def read_source(idx_ref, d, table_ref, w_ref, out_ref, low):
    own = (lax.broadcasted_iota(I32, (32, 256), 1) >> 3) == lax.broadcasted_iota(I32, (32, 256), 0)
    sums = []
    for g in range(4):
        patches = []
        for s in range(32):
            patches.append(table_ref[idx_ref[d, g * 32 + s]])
        weights = [jnp.where(own, w_ref[h, pl.ds(d, 1), g * 256:(g + 1) * 256], 0.0) for h in range(2)]
        sums.append(jnp.dot(
            jnp.concatenate(weights, axis=0).astype(BF16), jnp.concatenate(patches, axis=0).astype(BF16),
            preferred_element_type=F32))
    for g in range(2):
        first, second = sums[g], sums[g + 2]
        keep = jnp.where(low, first[:32], second[32:])
        move = jnp.where(low, second[:32], first[32:])
        at = pl.multiple_of(d * 64 + g * 32, 32)
        out_ref[pl.ds(at, 32), :] = (keep + pltpu.roll(move, 64, 1)).astype(BF16)


def place_body(idx_ref, half_ref, ret_ref, out_ref, wide_ref, x0_ref, x1_ref):
    rows = ret_ref.shape[0]

    def widen(k, _):
        at = pl.multiple_of(k * 256, 256)
        wide_ref[pl.ds(at, 256), :] = ret_ref[pl.ds(at, 256), :].astype(F32)
        return 0

    lax.fori_loop(0, rows // 256, widen, 0)

    def fetch(k, x_ref):
        for t in range(128):
            x_ref[t:t + 1, :] = wide_ref[pl.ds(idx_ref[k, t], 1), :]

    def work(k, x_ref):
        y = jnp.transpose(x_ref[...])
        second = half_ref[pl.ds(k, 1), :] > 0
        out_ref[:, pl.ds(pl.multiple_of(k * 128, 128), 128)] = jnp.where(second, y[64:], y[:64]).astype(BF16)

    blocks = half_ref.shape[0]
    fetch(0, x0_ref)

    def step(j, _):
        k = j * 2
        fetch(k + 1, x1_ref)
        work(k, x0_ref)
        fetch(jnp.minimum(k + 2, blocks - 1), x0_ref)
        work(k + 1, x1_ref)
        return 0

    lax.fori_loop(0, blocks // 2, step, 0)


def window_kernel(
    owner_ref, off_ref, fr_ref, grid_ref, tap_ref, gain_ref, up_ref, down_ref, read_ref, result_ref,
    hot_ref, val_ref, req_ref, got_ref, east_ref, west_ref, left_ref, right_ref, top_ref, bottom_ref, corner_ref,
    x_ref, tap8_ref, mix_ref, q_ref, row_ref, half_ref, idx_ref, where_ref, table_ref, w_ref, out_ref, ret_ref, wide_ref,
    x0_ref, x1_ref, idx_smem, row_smem,
    send_sem, recv_sem, req_send, req_recv, own_sem, val_send, val_recv, idx_sem, row_sem, *, n_lat, n_lon, turn, unroll):
    lat, lon = lax.axis_index("lat"), lax.axis_index("lon")
    me = lat * n_lon + lon
    devices = n_lat * n_lon
    tile_rows, tile_cols = grid_ref.shape[:2]
    first = lat * tile_rows - 1

    def partner(k):
        d = lax.rem(me + k * turn, devices)
        return d, (lax.div(d, n_lon), lax.rem(d, n_lon))

    barrier = pltpu.get_barrier_semaphore()

    def hello(k, _):
        pl.semaphore_signal(barrier, inc=1, device_id=partner(k)[1], device_id_type=pl.DeviceIdType.MESH)
        return 0

    lax.fori_loop(1, devices, hello, 0)

    def pack(k, _):
        a = grid_ref[2 * k].astype(F32)
        b = grid_ref[jnp.minimum(2 * k + 1, tile_rows - 1)].astype(F32)
        at = pl.ds(pl.multiple_of(k * 16, 16), 16)
        east_ref[at, :] = jnp.concatenate([a[tile_cols - 8:], b[tile_cols - 8:]], axis=0).astype(BF16)
        west_ref[at, :] = jnp.concatenate([a[:8], b[:8]], axis=0).astype(BF16)
        return 0

    pairs = (tile_rows + 1) // 2
    lax.fori_loop(0, pairs, pack, 0)
    up = lax.rem(lat + n_lat - 1, n_lat)
    down = lax.rem(lat + 1, n_lat)
    prev = lax.rem(lon + n_lon - 1, n_lon)
    post = lax.rem(lon + 1, n_lon)
    low_rows, high_rows = pl.ds((pairs - 3) * 16, 48), pl.ds(0, 48)
    moves = [
        (grid_ref.at[pl.ds(tile_rows - 4, 4)], top_ref, (down, lon)),
        (grid_ref.at[pl.ds(0, 5)], bottom_ref, (up, lon)),
        (east_ref, left_ref, (lat, post)),
        (west_ref, right_ref, (lat, prev)),
        (east_ref.at[low_rows], corner_ref.at[0], (down, post)),
        (west_ref.at[low_rows], corner_ref.at[1], (down, prev)),
        (east_ref.at[high_rows], corner_ref.at[2], (up, post)),
        (west_ref.at[high_rows], corner_ref.at[3], (up, prev)),
    ]
    halos = [
        pltpu.make_async_remote_copy(src_ref=a, dst_ref=b, send_sem=send_sem.at[n], recv_sem=recv_sem.at[n], device_id=to,
                                     device_id_type=pl.DeviceIdType.MESH)
        for n, (a, b, to) in enumerate(moves)
    ]
    route_body(owner_ref, off_ref, fr_ref, req_ref, row_ref, half_ref, hot_ref, val_ref)
    rows_in = pltpu.make_async_copy(row_ref, row_smem, row_sem)
    rows_in.start()
    pl.semaphore_wait(barrier, devices - 1)
    for h in halos:
        h.start()

    def eight(d):
        return pl.ds(pl.multiple_of(d * 8, 8), 8)

    own = pltpu.make_async_copy(req_ref.at[eight(me)], got_ref.at[eight(me)], own_sem)
    own.start()

    def ask(k, _):
        d, to = partner(k)
        pltpu.make_async_remote_copy(
            src_ref=req_ref.at[eight(d)], dst_ref=got_ref.at[eight(me)], send_sem=req_send, recv_sem=req_recv,
            device_id=to, device_id_type=pl.DeviceIdType.MESH).start()
        return 0

    lax.fori_loop(1, devices, ask, 0)

    def put(h, r, c, s, v):
        x_ref[h, pl.ds((r * EXT + c) * 8 + s, v.shape[0], stride=8), :] = v

    def put_row(r, s, v):
        for h in range(2):
            for c in range(0, tile_cols, 8):
                put(h, r, c + 8, s, v[c:min(c + 8, tile_cols), h * 128:(h + 1) * 128])

    def put_side(r, s, v, c):
        for h in range(2):
            put(h, r, c, s, v[:, h * 128:(h + 1) * 128])

    for r in range(12):
        if r >= 4:
            put_row(r, 0, grid_ref[r - 4].astype(F32))
        if r <= tile_rows - 39:
            put_row(r, 7, grid_ref[38 + r].astype(F32))

    def relay(r, _):
        for s in range(1, 7):
            put_row(r, s, grid_ref[6 * s + r - 4].astype(F32))
        return 0

    lax.fori_loop(0, 12, relay, 0)
    for h in range(2):
        for t in range(49):
            tap8_ref[h, t * 8:(t + 1) * 8, :] = jnp.broadcast_to(tap_ref[t:t + 1, h * 128:(h + 1) * 128].astype(F32), (8, 128))

    for h in halos:
        h.wait()
    above = jnp.where(lat > 0, 1.0, 0.0)
    below = jnp.where(lat < n_lat - 1, 1.0, 0.0)

    def block(ref, k):
        return ref[pl.ds(pl.multiple_of(k * 16, 16), 16), :].astype(F32)

    def sides(r2, s):
        k = 3 * s + r2 - 2
        a, b = block(left_ref, k), block(right_ref, k)
        for u in range(2):
            put_side(2 * r2 + u, s, a[8 * u:8 * u + 8], 0)
            put_side(2 * r2 + u, s, b[8 * u:8 * u + 8], tile_cols + 8)

    def middle(r2, _):
        for s in range(1, 7):
            sides(r2, s)
        return 0

    lax.fori_loop(0, 6, middle, 0)
    for r2 in range(2, 6):
        sides(r2, 0)
    for r2 in range(0, 4):
        sides(r2, 7)
    for r in range(4):
        put_row(r, 0, top_ref[r].astype(F32) * above)
        for n, c in ((0, 0), (1, tile_cols + 8)):
            v = corner_ref[n, (r + 1) // 2 * 16:(r + 1) // 2 * 16 + 16, :].astype(F32) * above
            put_side(r, 0, v[(r + 1) % 2 * 8:(r + 1) % 2 * 8 + 8], c)
    for r in range(7, 12):
        put_row(r, 7, bottom_ref[r - 7].astype(F32) * below)
        for n, c in ((2, 0), (3, tile_cols + 8)):
            v = corner_ref[n, (r - 7) // 2 * 16:(r - 7) // 2 * 16 + 16, :].astype(F32) * below
            put_side(r, 7, v[(r - 7) % 2 * 8:(r - 7) % 2 * 8 + 8], c)

    grid_body(x_ref, tap8_ref, mix_ref, gain_ref, up_ref, down_ref, read_ref, q_ref, first, tile_rows * n_lat)

    own.wait()
    most = pl.ds(0, (devices - 1) * 8)
    pltpu.make_async_copy(req_ref.at[most], got_ref.at[most], req_send).wait()
    pltpu.make_async_copy(req_ref.at[most], got_ref.at[most], req_recv).wait()
    cells = got_ref[pl.ds(0, devices, stride=8), :].astype(I32)
    idx_ref[...] = jnp.clip(cells, 0, tile_rows * tile_cols - 1)
    where_ref[0] = got_ref[pl.ds(1, devices, stride=8), :]
    where_ref[1] = got_ref[pl.ds(2, devices, stride=8), :]
    idx_in = pltpu.make_async_copy(idx_ref, idx_smem, idx_sem)
    idx_in.start()
    flat_weights(where_ref, w_ref)
    build_table(q_ref, table_ref, tile_rows, tile_cols)
    idx_in.wait()

    low = lax.broadcasted_iota(I32, (32, 128), 1) < 64

    def rows(d):
        return pl.ds(pl.multiple_of(d * 64, 64), 64)

    mine = pltpu.make_async_copy(out_ref.at[rows(me)], ret_ref.at[rows(me)], own_sem)

    def send(d, to):
        pltpu.make_async_remote_copy(
            src_ref=out_ref.at[rows(d)], dst_ref=ret_ref.at[rows(me)], send_sem=val_send, recv_sem=val_recv,
            device_id=to, device_id_type=pl.DeviceIdType.MESH).start()

    def serve(j, _):
        for u in range(unroll):
            d, to = partner(j * unroll + u)
            read_source(idx_smem, d, table_ref, w_ref, out_ref, low)
            if u:
                send(d, to)
            else:
                pl.when(j > 0)(functools.partial(send, d, to))
                pl.when(j == 0)(mine.start)
        return 0

    lax.fori_loop(0, devices // unroll, serve, 0)
    mine.wait()
    rows_in.wait()
    most = pl.ds(0, (devices - 1) * 64)
    pltpu.make_async_copy(out_ref.at[most], ret_ref.at[most], val_send).wait()
    pltpu.make_async_copy(out_ref.at[most], ret_ref.at[most], val_recv).wait()
    place_body(row_smem, half_ref, ret_ref, result_ref, wide_ref, x0_ref, x1_ref)


def window(owner, offsets, fractions, grid, taps, gain, up, down, read2, n_lat, n_lon):
    n = owner.shape[0] // 128
    devices = n_lat * n_lon
    tile_rows, tile_cols = grid.shape[:2]
    pairs = (tile_rows + 1) // 2
    dma = pltpu.SemaphoreType.DMA
    return pl.pallas_call(
        functools.partial(window_kernel, n_lat=n_lat, n_lon=n_lon, turn=37, unroll=8),
        out_shape=jax.ShapeDtypeStruct((64, n * 128), BF16),
        in_specs=[pl.BlockSpec(memory_space=VM)] * 9,
        out_specs=pl.BlockSpec(memory_space=VM),
        scratch_shapes=[
            VM((128, 1024), BF16), VM((768, 1024), BF16), VM((devices * 8, 128), F32), VM((devices * 8, 128), F32),
            VM((pairs * 16, 256), BF16), VM((pairs * 16, 256), BF16), VM((pairs * 16, 256), BF16), VM((pairs * 16, 256), BF16),
            VM((4, tile_cols, 256), BF16), VM((5, tile_cols, 256), BF16), VM((4, 48, 256), BF16),
            VM((2, 12 * EXT * 8, 128), F32), VM((2, 49 * 8, 128), F32), VM((6 * COLS * 8, 256), F32),
            VM((6 * COLS * 8, 128), F32), VM((n, 128), I32), VM((n, 128), I32), VM((devices, 128), I32), VM((2, devices, 128), F32),
            VM((tile_rows * tile_cols, 8, 128), F32), VM((2, devices, 1024), F32), VM((devices * 64, 128), BF16),
            VM((devices * 64, 128), BF16), VM((devices * 64, 128), F32), VM((128, 128), F32), VM((128, 128), F32),
            pltpu.SMEM((devices, 128), I32), pltpu.SMEM((n, 128), I32),
            dma((8,)), dma((8,)), dma, dma, dma, dma, dma, dma, dma],
        compiler_params=pltpu.CompilerParams(vmem_limit_bytes=60 << 20, has_side_effects=True, collective_id=0),
        name="window",
    )(owner.reshape(n, 128), offsets.reshape(n, 128), fractions, grid, taps, gain, up, down, read2)


def shards(grid, dw_kernel, norm_gain, w_up, w_down, w_read, owner, offsets, fractions):
    n_lat, n_lon = lax.axis_size("lat"), lax.axis_size("lon")
    read = w_read.T
    return window(
        owner, offsets, fractions, grid, dw_kernel.reshape(49, -1), norm_gain, w_up[0], w_down[0],
        jnp.concatenate([read, read], axis=0), n_lat, n_lon).T


def solution(mesh):
    return jax.shard_map(
        shards,
        mesh=mesh,
        in_specs=(P("lat", "lon", None), P(), P(), P(), P(), P(), P(("lat", "lon"), None), P(("lat", "lon")), P(None, ("lat", "lon"))),
        out_specs=P(("lat", "lon"), None),
        check_vma=False,
    )
```

```python
import functools
import jax, jax.numpy as jnp
from jax import lax
from jax.experimental import pallas as pl
from jax.experimental.pallas import tpu as pltpu
from jax.sharding import PartitionSpec as P
F32, BF16, I32 = jnp.float32, jnp.bfloat16, jnp.int32
VM = pltpu.VMEM

COLS, EXT = 96, 112
PAIRS = COLS // 2
SPLIT = 3


def route_body(owner_ref, off_ref, fr_ref, req_ref, row_ref, half_ref, hot_ref, val_ref):
    blocks = owner_ref.shape[0]
    sub = lax.broadcasted_iota(I32, (128, 128), 0)
    lane = lax.broadcasted_iota(I32, (128, 128), 1)
    upper = jnp.where(sub < lane, 1.0, 0.0).astype(BF16)
    prefix = jnp.concatenate([upper, jnp.ones((128, 128), BF16)], axis=1)
    group = 8

    def step(k, base):
        for u in range(group):
            b = k * group + u
            mine = owner_ref[pl.ds(b, 1), :]
            hot = jnp.where(mine == sub, 1.0, 0.0)
            hot16 = hot.astype(BF16)
            hot_ref[:, u * 128:(u + 1) * 128] = hot16
            sums = jnp.dot(hot16, prefix, preferred_element_type=F32)
            ranks = jnp.sum((sums[:, :128] + base) * hot, axis=0, keepdims=True)
            base = base + sums[:, 128:]
            rank = ranks.astype(I32)
            row_ref[pl.ds(b, 1), :] = jnp.clip(mine, 0, 127) * 64 + (rank & 63)
            half_ref[pl.ds(b, 1), :] = rank >> 6
            there = rank == sub
            off = off_ref[pl.ds(b, 1), :]
            fy = fr_ref[0:1, pl.ds(pl.multiple_of(b * 128, 128), 128)]
            fx = fr_ref[1:2, pl.ds(pl.multiple_of(b * 128, 128), 128)]
            fy_hi = fy.astype(BF16).astype(F32)
            fx_hi = fx.astype(BF16).astype(F32)
            parts = [(off >> 6).astype(F32), (off & 63).astype(F32), fy_hi, fy - fy_hi, fx_hi, fx - fx_hi]
            for p, part in enumerate(parts):
                val_ref[p * 128:(p + 1) * 128, u * 128:(u + 1) * 128] = jnp.where(there, part, 0.0).astype(BF16)
        acc = lax.dot_general(hot_ref[...], val_ref[...], (((1,), (1,)), ((), ())), preferred_element_type=F32)
        new = [acc[:, 0:128] * 64.0 + acc[:, 128:256], acc[:, 256:384] + acc[:, 384:512], acc[:, 512:640] + acc[:, 640:768]]
        for q in range(3):
            at = pl.ds(q, 128, stride=8)
            req_ref[at, :] = jnp.where(k == 0, new[q], req_ref[at, :] + new[q])
        return base

    lax.fori_loop(0, blocks // group, step, jnp.zeros((128, 128), F32))


def tap_bands(tap_ref, band_ref):
    eye = lax.broadcasted_iota(I32, (128, 128), 0) == lax.broadcasted_iota(I32, (128, 128), 1)
    for h in range(2):
        def fill(a, _):
            for j in range(8):
                for o in range(2):
                    if 0 <= j - o < 7:
                        taps = tap_ref[a, j - o:j - o + 1, h * 128:(h + 1) * 128].astype(F32)
                        block = jnp.where(eye, taps, 0.0).astype(BF16)
                    else:
                        block = jnp.zeros((128, 128), BF16)
                    band_ref[h, a, j * 128:(j + 1) * 128, o * 128:(o + 1) * 128] = block
            return 0

        lax.fori_loop(0, SPLIT, fill, 0)


def pack_pairs(x_ref, pack_ref):
    def step(r, _):
        for h in range(2):
            for par in range(2):
                for m in range(PAIRS // 2 + 2):
                    v = [x_ref[h, pl.ds(pl.multiple_of((r * EXT + 2 * (2 * m + n + 2) + par) * 8, 8), 8), :] for n in range(3)]
                    pack_ref[0, h, par, r, m * 16:m * 16 + 16, :] = jnp.concatenate(v[:2], axis=0).astype(BF16)
                    pack_ref[1, h, par, r, m * 16:m * 16 + 16, :] = jnp.concatenate(v[1:], axis=0).astype(BF16)
        return 0

    lax.fori_loop(0, 12, step, 0)


def conv_body(x_ref, tap8_ref, pack_ref, band_ref, part_ref, mix_ref, split):
    n = PAIRS * 8
    for h in range(2):
        def conv(r, _):
            for c0 in range(0, COLS, 6):
                acc = [None] * 6
                for a in range(split, 7):
                    x = [x_ref[h, pl.ds(pl.multiple_of(((r + a) * EXT + c0 + 4 + c) * 8, 8), 8), :] for c in range(12)]
                    for b in range(7):
                        k = tap8_ref[h, (a * 7 + b) * 8:(a * 7 + b) * 8 + 8, :]
                        for c in range(6):
                            p = x[c + b] * k
                            acc[c] = p if acc[c] is None else acc[c] + p
                for c in range(6):
                    part_ref[(c0 + c) % 2, (c0 + c) // 2 * 8:(c0 + c) // 2 * 8 + 8, :] = acc[c]
            acc = None
            for a in range(split):
                parts = []
                for q in range(4):
                    for par in range(2):
                        parts.append(pack_ref[q % 2, h, par, r + a, (q // 2) * 16:(q // 2) * 16 + n, :])
                p = jnp.dot(jnp.concatenate(parts, axis=1), band_ref[h, a], preferred_element_type=F32)
                acc = p if acc is None else acc + p
            for o in range(2):
                both = acc[:, o * 128:(o + 1) * 128] + part_ref[o]
                mix_ref[r, :, o, :, h * 128:(h + 1) * 128] = both.reshape(PAIRS, 8, 128)
            return 0

        lax.fori_loop(0, 6, conv, 0)


def grid_body(x_ref, tap8_ref, pack_ref, band_ref, part_ref, mix_ref, gain_ref, up_ref, down_ref, read_ref, q_ref, first, total_rows):
    conv_body(x_ref, tap8_ref, pack_ref, band_ref, part_ref, mix_ref, SPLIT)
    read = jnp.concatenate([read_ref[...], read_ref[...]], axis=0)
    n = COLS * 8
    low = lax.broadcasted_iota(I32, (n, 128), 1) < 64
    strip = lax.broadcasted_iota(I32, (n, 128), 0) & 7

    def mlp(r, _):
        at = pl.multiple_of(r * n, n)
        m = mix_ref[r].reshape(n, 256)
        m = m - jnp.mean(m, axis=1, keepdims=True)
        var = jnp.mean(m * m, axis=1, keepdims=True)
        normed = (m * lax.rsqrt(var + 1e-6) * gain_ref[...]).astype(BF16)
        hidden = jax.nn.gelu(jnp.dot(normed, up_ref[...], preferred_element_type=F32)).astype(BF16)
        delta = jnp.dot(hidden, down_ref[...], preferred_element_type=F32)
        mid = pl.multiple_of(((r + 3) * EXT + 7) * 8, 8)
        centre = jnp.concatenate([x_ref[0, pl.ds(mid, n), :], x_ref[1, pl.ds(mid, n), :]], axis=1)
        field = (centre + delta).astype(BF16)
        p = lax.dot_general(field, read, (((1,), (1,)), ((), ())), preferred_element_type=F32)
        p = p.astype(BF16).astype(F32)
        row = first + strip * 6 + r
        p = jnp.where((row >= 0) & (row < total_rows), p, 0.0)
        q_ref[pl.ds(at, n), :] = jnp.where(low, p, jnp.concatenate([p[8:], p[:8]], axis=0))
        return 0

    lax.fori_loop(0, 6, mlp, 0)


def flat_weights(fr_ref, w_ref):
    fy, fx = fr_ref[0], fr_ref[1]
    a = [jnp.exp(-fy - 0.5), jnp.ones_like(fy), jnp.exp(fy - 0.5), jnp.exp(fy + fy - 2.0)]
    b = [jnp.exp(-fx - 0.5), jnp.ones_like(fx), jnp.exp(fx - 0.5), jnp.exp(fx + fx - 2.0)]
    scale = 1.0 / ((a[0] + a[1] + a[2] + a[3]) * (b[0] + b[1] + b[2] + b[3]))
    a = [x * scale for x in a]
    row = lax.broadcasted_iota(I32, (128, 1024), 0)
    col = lax.broadcasted_iota(I32, (128, 1024), 1)
    for s in range(8):
        one = jnp.where(col == row * 8 + s, 1.0, 0.0).astype(BF16)
        for half in range(2):
            plane = (a[s // 2] * b[2 * (s % 2) + half]).astype(BF16)
            part = jnp.dot(plane, one, preferred_element_type=F32)
            w_ref[half] = part if s == 0 else w_ref[half] + part


def build_table(q_ref, table_ref, tile_rows, tile_cols):
    sub = lax.broadcasted_iota(I32, (8, 128), 0)
    masks = {n: (sub & n) == 0 for n in (1, 2, 4)}

    def build(c, _):
        q = [[None] * 2 for _ in range(9)]
        for jj in range(2):
            for r in range(6):
                q[r][jj] = q_ref[pl.ds(pl.multiple_of((r * COLS + c + 2 * jj) * 8, 8), 8), :]
            for r in range(3):
                q[r + 6][jj] = pltpu.roll(q[r][jj], 7, 0)
        for r in range(6):
            v = [q[r + i][jj] for i in range(4) for jj in range(2)]
            for n in (4, 2, 1):
                new = list(v)
                for k in range(8):
                    if not k & n:
                        new[k] = jnp.where(masks[n], v[k], pltpu.roll(v[k + n], n, 0))
                        new[k + n] = jnp.where(masks[n], pltpu.roll(v[k], 8 - n, 0), v[k + n])
                v = new
            for k in range(8):
                if 6 * k + r < tile_rows:
                    table_ref[(6 * k + r) * tile_cols + c] = v[k]
        return 0

    lax.fori_loop(0, tile_cols, build, 0)


def read_source(idx_ref, d, table_ref, w_ref, out_ref, low):
    own = (lax.broadcasted_iota(I32, (32, 256), 1) >> 3) == lax.broadcasted_iota(I32, (32, 256), 0)
    sums = []
    for g in range(4):
        patches = []
        for s in range(32):
            patches.append(table_ref[idx_ref[d, g * 32 + s]])
        weights = [jnp.where(own, w_ref[h, pl.ds(d, 1), g * 256:(g + 1) * 256], 0.0) for h in range(2)]
        sums.append(jnp.dot(
            jnp.concatenate(weights, axis=0).astype(BF16), jnp.concatenate(patches, axis=0).astype(BF16),
            preferred_element_type=F32))
    for g in range(2):
        first, second = sums[g], sums[g + 2]
        keep = jnp.where(low, first[:32], second[32:])
        move = jnp.where(low, second[:32], first[32:])
        at = pl.multiple_of(d * 64 + g * 32, 32)
        out_ref[pl.ds(at, 32), :] = (keep + pltpu.roll(move, 64, 1)).astype(BF16)


def place_body(idx_ref, half_ref, wide_ref, out_ref, x0_ref, x1_ref):
    def fetch(k, x_ref):
        for t in range(128):
            x_ref[t:t + 1, :] = wide_ref[pl.ds(idx_ref[k, t], 1), :]

    def work(k, x_ref):
        y = jnp.transpose(x_ref[...])
        second = half_ref[pl.ds(k, 1), :] > 0
        out_ref[:, pl.ds(pl.multiple_of(k * 128, 128), 128)] = jnp.where(second, y[64:], y[:64]).astype(BF16)

    blocks = half_ref.shape[0]
    fetch(0, x0_ref)

    def step(j, _):
        k = j * 2
        fetch(k + 1, x1_ref)
        work(k, x0_ref)
        fetch(jnp.minimum(k + 2, blocks - 1), x0_ref)
        work(k + 1, x1_ref)
        return 0

    lax.fori_loop(0, blocks // 2, step, 0)


def window_kernel(
    owner_ref, off_ref, fr_ref, grid_ref, tap_ref, gain_ref, up_ref, down_ref, read_ref, result_ref,
    hot_ref, val_ref, req_ref, got_ref, east_ref, west_ref, left_ref, right_ref, top_ref, bottom_ref, corner_ref,
    x_ref, tap8_ref, pack_ref, band_ref, part_ref, mix_ref, q_ref, row_ref, half_ref, idx_ref, where_ref, table_ref, w_ref, out_ref, ret_ref,
    x0_ref, x1_ref, idx_smem, row_smem,
    send_sem, recv_sem, req_send, req_recv, own_sem, val_send, val_recv, idx_sem, row_sem, *, n_lat, n_lon, turn, unroll):
    lat, lon = lax.axis_index("lat"), lax.axis_index("lon")
    me = lat * n_lon + lon
    devices = n_lat * n_lon
    tile_rows, tile_cols = grid_ref.shape[:2]
    first = lat * tile_rows - 1

    def partner(k):
        d = lax.rem(me + k * turn, devices)
        return d, (lax.div(d, n_lon), lax.rem(d, n_lon))

    barrier = pltpu.get_barrier_semaphore()

    def hello(k, _):
        pl.semaphore_signal(barrier, inc=1, device_id=partner(k)[1], device_id_type=pl.DeviceIdType.MESH)
        return 0

    lax.fori_loop(1, devices, hello, 0)

    def pack(k, _):
        a = grid_ref[2 * k].astype(F32)
        b = grid_ref[jnp.minimum(2 * k + 1, tile_rows - 1)].astype(F32)
        at = pl.ds(pl.multiple_of(k * 16, 16), 16)
        east_ref[at, :] = jnp.concatenate([a[tile_cols - 8:], b[tile_cols - 8:]], axis=0).astype(BF16)
        west_ref[at, :] = jnp.concatenate([a[:8], b[:8]], axis=0).astype(BF16)
        return 0

    pairs = (tile_rows + 1) // 2
    lax.fori_loop(0, pairs, pack, 0)
    up = lax.rem(lat + n_lat - 1, n_lat)
    down = lax.rem(lat + 1, n_lat)
    prev = lax.rem(lon + n_lon - 1, n_lon)
    post = lax.rem(lon + 1, n_lon)
    low_rows, high_rows = pl.ds((pairs - 3) * 16, 48), pl.ds(0, 48)
    moves = [
        (grid_ref.at[pl.ds(tile_rows - 4, 4)], top_ref, (down, lon)),
        (grid_ref.at[pl.ds(0, 5)], bottom_ref, (up, lon)),
        (east_ref, left_ref, (lat, post)),
        (west_ref, right_ref, (lat, prev)),
        (east_ref.at[low_rows], corner_ref.at[0], (down, post)),
        (west_ref.at[low_rows], corner_ref.at[1], (down, prev)),
        (east_ref.at[high_rows], corner_ref.at[2], (up, post)),
        (west_ref.at[high_rows], corner_ref.at[3], (up, prev)),
    ]
    halos = [
        pltpu.make_async_remote_copy(src_ref=a, dst_ref=b, send_sem=send_sem.at[n], recv_sem=recv_sem.at[n], device_id=to,
                                     device_id_type=pl.DeviceIdType.MESH)
        for n, (a, b, to) in enumerate(moves)
    ]
    route_body(owner_ref, off_ref, fr_ref, req_ref, row_ref, half_ref, hot_ref, val_ref)
    rows_in = pltpu.make_async_copy(row_ref, row_smem, row_sem)
    rows_in.start()
    pl.semaphore_wait(barrier, devices - 1)
    for h in halos:
        h.start()

    def eight(d):
        return pl.ds(pl.multiple_of(d * 8, 8), 8)

    own = pltpu.make_async_copy(req_ref.at[eight(me)], got_ref.at[eight(me)], own_sem)
    own.start()

    def ask(k, _):
        d, to = partner(k)
        pltpu.make_async_remote_copy(
            src_ref=req_ref.at[eight(d)], dst_ref=got_ref.at[eight(me)], send_sem=req_send, recv_sem=req_recv,
            device_id=to, device_id_type=pl.DeviceIdType.MESH).start()
        return 0

    lax.fori_loop(1, devices, ask, 0)

    def put(h, r, c, s, v):
        x_ref[h, pl.ds((r * EXT + c) * 8 + s, v.shape[0], stride=8), :] = v

    def put_row(r, s, v):
        for h in range(2):
            for c in range(0, tile_cols, 8):
                put(h, r, c + 8, s, v[c:min(c + 8, tile_cols), h * 128:(h + 1) * 128])

    def put_side(r, s, v, c):
        for h in range(2):
            put(h, r, c, s, v[:, h * 128:(h + 1) * 128])

    for r in range(12):
        if r >= 4:
            put_row(r, 0, grid_ref[r - 4].astype(F32))
        if r <= tile_rows - 39:
            put_row(r, 7, grid_ref[38 + r].astype(F32))

    def relay(r, _):
        for s in range(1, 7):
            put_row(r, s, grid_ref[6 * s + r - 4].astype(F32))
        return 0

    lax.fori_loop(0, 12, relay, 0)
    for h in range(2):
        for t in range(7 * SPLIT, 49):
            tap8_ref[h, t * 8:(t + 1) * 8, :] = jnp.broadcast_to(tap_ref[t // 7, t % 7:t % 7 + 1, h * 128:(h + 1) * 128].astype(F32), (8, 128))

    tap_bands(tap_ref, band_ref)

    for h in halos:
        h.wait()
    above = jnp.where(lat > 0, 1.0, 0.0)
    below = jnp.where(lat < n_lat - 1, 1.0, 0.0)

    def block(ref, k):
        return ref[pl.ds(pl.multiple_of(k * 16, 16), 16), :].astype(F32)

    def sides(r2, s):
        k = 3 * s + r2 - 2
        a, b = block(left_ref, k), block(right_ref, k)
        for u in range(2):
            put_side(2 * r2 + u, s, a[8 * u:8 * u + 8], 0)
            put_side(2 * r2 + u, s, b[8 * u:8 * u + 8], tile_cols + 8)

    def middle(r2, _):
        for s in range(1, 7):
            sides(r2, s)
        return 0

    lax.fori_loop(0, 6, middle, 0)
    for r2 in range(2, 6):
        sides(r2, 0)
    for r2 in range(0, 4):
        sides(r2, 7)
    for r in range(4):
        put_row(r, 0, top_ref[r].astype(F32) * above)
        for n, c in ((0, 0), (1, tile_cols + 8)):
            v = corner_ref[n, (r + 1) // 2 * 16:(r + 1) // 2 * 16 + 16, :].astype(F32) * above
            put_side(r, 0, v[(r + 1) % 2 * 8:(r + 1) % 2 * 8 + 8], c)
    for r in range(7, 12):
        put_row(r, 7, bottom_ref[r - 7].astype(F32) * below)
        for n, c in ((2, 0), (3, tile_cols + 8)):
            v = corner_ref[n, (r - 7) // 2 * 16:(r - 7) // 2 * 16 + 16, :].astype(F32) * below
            put_side(r, 7, v[(r - 7) % 2 * 8:(r - 7) % 2 * 8 + 8], c)

    pack_pairs(x_ref, pack_ref)
    grid_body(x_ref, tap8_ref, pack_ref, band_ref, part_ref, mix_ref, gain_ref, up_ref, down_ref, read_ref, q_ref, first, tile_rows * n_lat)

    own.wait()
    most = pl.ds(0, (devices - 1) * 8)
    pltpu.make_async_copy(req_ref.at[most], got_ref.at[most], req_send).wait()
    pltpu.make_async_copy(req_ref.at[most], got_ref.at[most], req_recv).wait()
    cells = got_ref[pl.ds(0, devices, stride=8), :].astype(I32)
    idx_ref[...] = jnp.clip(cells, 0, tile_rows * tile_cols - 1)
    where_ref[0] = got_ref[pl.ds(1, devices, stride=8), :]
    where_ref[1] = got_ref[pl.ds(2, devices, stride=8), :]
    idx_in = pltpu.make_async_copy(idx_ref, idx_smem, idx_sem)
    idx_in.start()
    flat_weights(where_ref, w_ref)
    build_table(q_ref, table_ref, tile_rows, tile_cols)
    idx_in.wait()

    low = lax.broadcasted_iota(I32, (32, 128), 1) < 64

    share = devices // 8

    def rows(d):
        return pl.ds(pl.multiple_of(d * 64, 64), 64)

    mine = pltpu.make_async_copy(out_ref.at[rows(me)], ret_ref.at[rows(me)], own_sem)

    def send(d, to, group):
        pltpu.make_async_remote_copy(
            src_ref=out_ref.at[rows(d)], dst_ref=ret_ref.at[rows(me)], send_sem=val_send, recv_sem=val_recv.at[group],
            device_id=to, device_id_type=pl.DeviceIdType.MESH).start()

    def serve(j, _):
        those = [partner(j * unroll + u) for u in range(unroll)]
        for d, _ in those:
            read_source(idx_smem, d, table_ref, w_ref, out_ref, low)
        group = lax.div(j * unroll, share)
        pl.when(j > 0)(functools.partial(send, *those[0], group))
        pl.when(j == 0)(mine.start)
        for d, to in those[1:]:
            send(d, to, group)
        return 0

    lax.fori_loop(0, devices // unroll, serve, 0)
    wide_ref = x_ref.at[0]
    for group in range(devices // share):
        count = pl.ds(0, (share - (group == 0)) * 64)
        pltpu.make_async_copy(out_ref.at[count], ret_ref.at[count], val_recv.at[group]).wait()
        if group == 0:
            mine.wait()

        def widen(k, _):
            s = lax.rem(me + (devices - k) * turn, devices)
            wide_ref[rows(s), :] = ret_ref[rows(s), :].astype(F32)
            return 0

        lax.fori_loop(group * share, (group + 1) * share, widen, 0)

    rows_in.wait()
    most = pl.ds(0, (devices - 1) * 64)
    pltpu.make_async_copy(out_ref.at[most], ret_ref.at[most], val_send).wait()
    place_body(row_smem, half_ref, wide_ref, result_ref, x0_ref, x1_ref)


def window(owner, offsets, fractions, grid, taps, gain, up, down, read2, n_lat, n_lon):
    n = owner.shape[0] // 128
    devices = n_lat * n_lon
    tile_rows, tile_cols = grid.shape[:2]
    pairs = (tile_rows + 1) // 2
    dma = pltpu.SemaphoreType.DMA
    return pl.pallas_call(
        functools.partial(window_kernel, n_lat=n_lat, n_lon=n_lon, turn=37, unroll=8),
        out_shape=jax.ShapeDtypeStruct((64, n * 128), BF16),
        in_specs=[pl.BlockSpec(memory_space=VM)] * 9,
        out_specs=pl.BlockSpec(memory_space=VM),
        scratch_shapes=[
            VM((128, 1024), BF16), VM((768, 1024), BF16), VM((devices * 8, 128), F32), VM((devices * 8, 128), F32),
            VM((pairs * 16, 256), BF16), VM((pairs * 16, 256), BF16), VM((pairs * 16, 256), BF16), VM((pairs * 16, 256), BF16),
            VM((4, tile_cols, 256), BF16), VM((5, tile_cols, 256), BF16), VM((4, 48, 256), BF16),
            VM((2, 12 * EXT * 8, 128), F32), VM((2, 49 * 8, 128), F32),
            VM((2, 2, 2, 12, PAIRS * 8 + 32, 128), BF16), VM((2, SPLIT, 1024, 256), BF16), VM((2, PAIRS * 8, 128), F32),
            VM((6, PAIRS, 2, 8, 256), F32),
            VM((6 * COLS * 8, 128), F32), VM((n, 128), I32), VM((n, 128), I32), VM((devices, 128), I32), VM((2, devices, 128), F32),
            VM((tile_rows * tile_cols, 8, 128), F32), VM((2, devices, 1024), F32), VM((devices * 64, 128), BF16),
            VM((devices * 64, 128), BF16), VM((128, 128), F32), VM((128, 128), F32),
            pltpu.SMEM((devices, 128), I32), pltpu.SMEM((n, 128), I32),
            dma((8,)), dma((8,)), dma, dma, dma, dma, dma((8,)), dma, dma],
        compiler_params=pltpu.CompilerParams(vmem_limit_bytes=62 << 20, has_side_effects=True, collective_id=0),
        name="window",
    )(owner.reshape(n, 128), offsets.reshape(n, 128), fractions, grid, taps, gain, up, down, read2)


def shards(grid, dw_kernel, norm_gain, w_up, w_down, w_read, owner, offsets, fractions):
    n_lat, n_lon = lax.axis_size("lat"), lax.axis_size("lon")
    return window(
        owner, offsets, fractions, grid, dw_kernel[0], norm_gain, w_up[0], w_down[0],
        w_read.T, n_lat, n_lon).T


def solution(mesh):
    return jax.shard_map(
        shards,
        mesh=mesh,
        in_specs=(P("lat", "lon", None), P(), P(), P(), P(), P(), P(("lat", "lon"), None), P(("lat", "lon")), P(None, ("lat", "lon"))),
        out_specs=P(("lat", "lon"), None),
        check_vma=False,
    )
```

```python
import functools
import jax, jax.numpy as jnp
from jax import lax
from jax.experimental import pallas as pl
from jax.experimental.pallas import tpu as pltpu
from jax.sharding import PartitionSpec as P
F32, BF16, I32 = jnp.float32, jnp.bfloat16, jnp.int32
VM = pltpu.VMEM

COLS, EXT = 96, 112
PAIRS = COLS // 2
SPLIT = 3


def route_body(owner_ref, off_ref, fr_ref, req_ref, row_ref, half_ref, hot_ref, val_ref, sum_ref):
    blocks = owner_ref.shape[0]
    sub = lax.broadcasted_iota(I32, (128, 128), 0)
    lane = lax.broadcasted_iota(I32, (128, 128), 1)
    upper = jnp.where(sub < lane, 1.0, 0.0).astype(BF16)
    prefix = jnp.concatenate([upper, jnp.ones((128, 128), BF16)], axis=1)
    group = 16

    def step(k, base):
        for u in range(group):
            b = k * group + u
            mine = owner_ref[pl.ds(b, 1), :]
            hot = jnp.where(mine == sub, 1.0, 0.0)
            hot16 = hot.astype(BF16)
            hot_ref[:, u * 128:(u + 1) * 128] = hot16
            sums = jnp.dot(hot16, prefix, preferred_element_type=F32)
            ranks = jnp.sum((sums[:, :128] + base) * hot, axis=0, keepdims=True)
            base = base + sums[:, 128:]
            rank = ranks.astype(I32)
            row_ref[pl.ds(b, 1), :] = jnp.clip(mine, 0, 127) * 64 + (rank & 63)
            half_ref[pl.ds(b, 1), :] = rank >> 6
            there = rank == sub
            off = off_ref[pl.ds(b, 1), :]
            fy = fr_ref[0:1, pl.ds(pl.multiple_of(b * 128, 128), 128)]
            fx = fr_ref[1:2, pl.ds(pl.multiple_of(b * 128, 128), 128)]
            fy_hi = fy.astype(BF16).astype(F32)
            fx_hi = fx.astype(BF16).astype(F32)
            parts = [(off >> 6).astype(F32), (off & 63).astype(F32), fy_hi, fy - fy_hi, fx_hi, fx - fx_hi]
            for p, part in enumerate(parts):
                val_ref[p * 128:(p + 1) * 128, u * 128:(u + 1) * 128] = jnp.where(there, part, 0.0).astype(BF16)
        acc = lax.dot_general(val_ref[...], hot_ref[...], (((1,), (1,)), ((), ())), preferred_element_type=F32)
        new = [acc[0:128] * 64.0 + acc[128:256], acc[256:384] + acc[384:512], acc[512:640] + acc[640:768]]
        for q in range(3):
            sum_ref[q] = jnp.where(k == 0, new[q], sum_ref[q] + new[q])
        return base

    lax.fori_loop(0, blocks // group, step, jnp.zeros((128, 128), F32))
    for q in range(3):
        req_ref[pl.ds(q, 128, stride=8), :] = jnp.transpose(sum_ref[q])


def tap_bands(tap_ref, band_ref):
    eye = lax.broadcasted_iota(I32, (128, 128), 0) == lax.broadcasted_iota(I32, (128, 128), 1)
    for h in range(2):
        def fill(a, _):
            for j in range(8):
                for o in range(2):
                    if 0 <= j - o < 7:
                        taps = tap_ref[a, j - o:j - o + 1, h * 128:(h + 1) * 128].astype(F32)
                        block = jnp.where(eye, taps, 0.0).astype(BF16)
                    else:
                        block = jnp.zeros((128, 128), BF16)
                    band_ref[h, a, j * 128:(j + 1) * 128, o * 128:(o + 1) * 128] = block
            return 0

        lax.fori_loop(0, SPLIT, fill, 0)


def pack_pairs(x_ref, pack_ref):
    def step(r, _):
        for h in range(2):
            for par in range(2):
                for m in range(PAIRS // 2 + 2):
                    v = [x_ref[h, pl.ds(pl.multiple_of((r * EXT + 2 * (2 * m + n + 2) + par) * 8, 8), 8), :] for n in range(3)]
                    pack_ref[0, h, par, r, m * 16:m * 16 + 16, :] = jnp.concatenate(v[:2], axis=0).astype(BF16)
                    pack_ref[1, h, par, r, m * 16:m * 16 + 16, :] = jnp.concatenate(v[1:], axis=0).astype(BF16)
        return 0

    lax.fori_loop(0, 12, step, 0)


def conv_body(x_ref, tap8_ref, pack_ref, band_ref, part_ref, mix_ref, split):
    n = PAIRS * 8
    for h in range(2):
        def conv(r, _):
            for c0 in range(0, COLS, 6):
                acc = [None] * 6
                for a in range(split, 7):
                    x = [x_ref[h, pl.ds(pl.multiple_of(((r + a) * EXT + c0 + 4 + c) * 8, 8), 8), :] for c in range(12)]
                    for b in range(7):
                        k = tap8_ref[h, (a * 7 + b) * 8:(a * 7 + b) * 8 + 8, :]
                        for c in range(6):
                            p = x[c + b] * k
                            acc[c] = p if acc[c] is None else acc[c] + p
                for c in range(6):
                    part_ref[(c0 + c) % 2, (c0 + c) // 2 * 8:(c0 + c) // 2 * 8 + 8, :] = acc[c]
            acc = None
            for a in range(split):
                parts = []
                for q in range(4):
                    for par in range(2):
                        parts.append(pack_ref[q % 2, h, par, r + a, (q // 2) * 16:(q // 2) * 16 + n, :])
                p = jnp.dot(jnp.concatenate(parts, axis=1), band_ref[h, a], preferred_element_type=F32)
                acc = p if acc is None else acc + p
            for o in range(2):
                both = acc[:, o * 128:(o + 1) * 128] + part_ref[o]
                mix_ref[r, :, o, :, h * 128:(h + 1) * 128] = both.reshape(PAIRS, 8, 128)
            return 0

        lax.fori_loop(0, 6, conv, 0)


def grid_body(x_ref, tap8_ref, pack_ref, band_ref, part_ref, mix_ref, gain_ref, up_ref, down_ref, read_ref, q_ref, first, total_rows):
    conv_body(x_ref, tap8_ref, pack_ref, band_ref, part_ref, mix_ref, SPLIT)
    read = jnp.concatenate([read_ref[...], read_ref[...]], axis=0)
    n = COLS * 8
    low = lax.broadcasted_iota(I32, (n, 128), 1) < 64
    strip = lax.broadcasted_iota(I32, (n, 128), 0) & 7

    def mlp(r, _):
        at = pl.multiple_of(r * n, n)
        m = mix_ref[r].reshape(n, 256)
        m = m - jnp.mean(m, axis=1, keepdims=True)
        var = jnp.mean(m * m, axis=1, keepdims=True)
        normed = (m * lax.rsqrt(var + 1e-6) * gain_ref[...]).astype(BF16)
        hidden = jax.nn.gelu(jnp.dot(normed, up_ref[...], preferred_element_type=F32)).astype(BF16)
        delta = jnp.dot(hidden, down_ref[...], preferred_element_type=F32)
        mid = pl.multiple_of(((r + 3) * EXT + 7) * 8, 8)
        centre = jnp.concatenate([x_ref[0, pl.ds(mid, n), :], x_ref[1, pl.ds(mid, n), :]], axis=1)
        field = (centre + delta).astype(BF16)
        p = lax.dot_general(field, read, (((1,), (1,)), ((), ())), preferred_element_type=F32)
        p = p.astype(BF16).astype(F32)
        row = first + strip * 6 + r
        p = jnp.where((row >= 0) & (row < total_rows), p, 0.0)
        q_ref[pl.ds(at, n), :] = jnp.where(low, p, jnp.concatenate([p[8:], p[:8]], axis=0))
        return 0

    lax.fori_loop(0, 6, mlp, 0)


def flat_weights(fr_ref, w_ref):
    fy, fx = fr_ref[0], fr_ref[1]
    a = [jnp.exp(-fy - 0.5), jnp.ones_like(fy), jnp.exp(fy - 0.5), jnp.exp(fy + fy - 2.0)]
    b = [jnp.exp(-fx - 0.5), jnp.ones_like(fx), jnp.exp(fx - 0.5), jnp.exp(fx + fx - 2.0)]
    scale = 1.0 / ((a[0] + a[1] + a[2] + a[3]) * (b[0] + b[1] + b[2] + b[3]))
    a = [x * scale for x in a]
    row = lax.broadcasted_iota(I32, (128, 1024), 0)
    col = lax.broadcasted_iota(I32, (128, 1024), 1)
    for s in range(8):
        one = jnp.where(col == row * 8 + s, 1.0, 0.0).astype(BF16)
        planes = [(a[s // 2] * b[2 * (s % 2) + half]).astype(BF16) for half in range(2)]
        part = jnp.dot(jnp.concatenate(planes, axis=0), one, preferred_element_type=F32)
        for half in range(2):
            own = part[half * 128:(half + 1) * 128]
            w_ref[half] = own if s == 0 else w_ref[half] + own


def build_table(q_ref, table_ref, tile_rows, tile_cols):
    sub = lax.broadcasted_iota(I32, (8, 128), 0)
    masks = {n: (sub & n) == 0 for n in (1, 2, 4)}

    def build(c, _):
        q = [[None] * 2 for _ in range(9)]
        for jj in range(2):
            for r in range(6):
                q[r][jj] = q_ref[pl.ds(pl.multiple_of((r * COLS + c + 2 * jj) * 8, 8), 8), :]
            for r in range(3):
                q[r + 6][jj] = pltpu.roll(q[r][jj], 7, 0)
        for r in range(6):
            v = [q[r + i][jj] for i in range(4) for jj in range(2)]
            for n in (4, 2, 1):
                new = list(v)
                for k in range(8):
                    if not k & n:
                        new[k] = jnp.where(masks[n], v[k], pltpu.roll(v[k + n], n, 0))
                        new[k + n] = jnp.where(masks[n], pltpu.roll(v[k], 8 - n, 0), v[k + n])
                v = new
            for k in range(8):
                if 6 * k + r < tile_rows:
                    table_ref[(6 * k + r) * tile_cols + c] = v[k]
        return 0

    lax.fori_loop(0, tile_cols, build, 0)


def read_source(idx_ref, d, table_ref, w_ref, out_ref, low):
    own = (lax.broadcasted_iota(I32, (32, 256), 1) >> 3) == lax.broadcasted_iota(I32, (32, 256), 0)
    sums = []
    for g in range(4):
        patches = []
        for s in range(32):
            patches.append(table_ref[idx_ref[d, g * 32 + s]])
        weights = [jnp.where(own, w_ref[h, pl.ds(d, 1), g * 256:(g + 1) * 256], 0.0) for h in range(2)]
        sums.append(jnp.dot(
            jnp.concatenate(weights, axis=0).astype(BF16), jnp.concatenate(patches, axis=0).astype(BF16),
            preferred_element_type=F32))
    for g in range(2):
        first, second = sums[g], sums[g + 2]
        keep = jnp.where(low, first[:32], second[32:])
        move = jnp.where(low, second[:32], first[32:])
        at = pl.multiple_of(d * 64 + g * 32, 32)
        out_ref[pl.ds(at, 32), :] = (keep + pltpu.roll(move, 64, 1)).astype(BF16)


def place_body(idx_ref, half_ref, wide_ref, out_ref, x0_ref, x1_ref):
    def fetch(k, x_ref):
        for t in range(128):
            x_ref[t:t + 1, :] = wide_ref[pl.ds(idx_ref[k, t], 1), :]

    def work(k, x_ref):
        y = jnp.transpose(x_ref[...])
        second = half_ref[pl.ds(k, 1), :] > 0
        out_ref[:, pl.ds(pl.multiple_of(k * 128, 128), 128)] = jnp.where(second, y[64:], y[:64]).astype(BF16)

    blocks = half_ref.shape[0]
    fetch(0, x0_ref)

    def step(j, _):
        k = j * 2
        fetch(k + 1, x1_ref)
        work(k, x0_ref)
        fetch(jnp.minimum(k + 2, blocks - 1), x0_ref)
        work(k + 1, x1_ref)
        return 0

    lax.fori_loop(0, blocks // 2, step, 0)


def window_kernel(
    owner_ref, off_ref, fr_ref, grid_hbm, tap_ref, gain_ref, up_ref, down_ref, read_ref, result_ref,
    grid_ref, hot_ref, val_ref, sum_ref, req_ref, got_ref, east_ref, west_ref, left_ref, right_ref, top_ref, bottom_ref, corner_ref,
    x_ref, tap8_ref, pack_ref, band_ref, part_ref, mix_ref, q_ref, row_ref, half_ref, idx_ref, where_ref, table_ref, w_ref, out_ref, ret_ref,
    x0_ref, x1_ref, idx_smem, row_smem,
    send_sem, recv_sem, req_send, req_recv, own_sem, val_send, val_recv, idx_sem, row_sem, grid_sem, line_sem, *, n_lat, n_lon, turn, unroll):
    lat, lon = lax.axis_index("lat"), lax.axis_index("lon")
    me = lat * n_lon + lon
    devices = n_lat * n_lon
    tile_rows, tile_cols = grid_ref.shape[:2]
    first = lat * tile_rows - 1

    def partner(k):
        d = lax.rem(me + k * turn, devices)
        return d, (lax.div(d, n_lon), lax.rem(d, n_lon))

    barrier = pltpu.get_barrier_semaphore()

    def greet(sem, to):
        pl.semaphore_signal(sem, inc=1, device_id=to, device_id_type=pl.DeviceIdType.MESH)

    for k in range(1, n_lon):
        greet(barrier, (lat, lax.rem(lon + k, n_lon)))
    for k in range(1, n_lat):
        greet(barrier, (lax.rem(lat + k, n_lat), lon))
    grid_in = pltpu.make_async_copy(grid_hbm, grid_ref, grid_sem)
    grid_in.start()

    pairs = (tile_rows + 1) // 2
    up = lax.rem(lat + n_lat - 1, n_lat)
    down = lax.rem(lat + 1, n_lat)
    prev = lax.rem(lon + n_lon - 1, n_lon)
    post = lax.rem(lon + 1, n_lon)
    low_rows, high_rows = pl.ds((pairs - 3) * 16, 48), pl.ds(0, 48)
    moves = [
        (grid_ref.at[pl.ds(tile_rows - 4, 4)], top_ref, (down, lon)),
        (grid_ref.at[pl.ds(0, 5)], bottom_ref, (up, lon)),
        (east_ref, left_ref, (lat, post)),
        (west_ref, right_ref, (lat, prev)),
        (east_ref.at[low_rows], corner_ref.at[0], (down, post)),
        (west_ref.at[low_rows], corner_ref.at[1], (down, prev)),
        (east_ref.at[high_rows], corner_ref.at[2], (up, post)),
        (west_ref.at[high_rows], corner_ref.at[3], (up, prev)),
    ]
    halos = [
        pltpu.make_async_remote_copy(src_ref=a, dst_ref=b, send_sem=send_sem.at[n], recv_sem=recv_sem.at[n], device_id=to,
                                     device_id_type=pl.DeviceIdType.MESH)
        for n, (a, b, to) in enumerate(moves)
    ]
    route_body(owner_ref, off_ref, fr_ref, req_ref, row_ref, half_ref, hot_ref, val_ref, sum_ref)
    rows_in = pltpu.make_async_copy(row_ref, row_smem, row_sem)
    rows_in.start()
    pl.semaphore_wait(barrier, n_lat + n_lon - 2)
    for k in range(1, n_lat):
        greet(line_sem, (lax.rem(lat + k, n_lat), lon))
    grid_in.wait()
    def pack(k, _):
        a = grid_ref[2 * k].astype(F32)
        b = grid_ref[jnp.minimum(2 * k + 1, tile_rows - 1)].astype(F32)
        at = pl.ds(pl.multiple_of(k * 16, 16), 16)
        east_ref[at, :] = jnp.concatenate([a[tile_cols - 8:], b[tile_cols - 8:]], axis=0).astype(BF16)
        west_ref[at, :] = jnp.concatenate([a[:8], b[:8]], axis=0).astype(BF16)
        return 0

    lax.fori_loop(0, pairs, pack, 0)

    def put(h, r, c, s, v):
        x_ref[h, pl.ds((r * EXT + c) * 8 + s, v.shape[0], stride=8), :] = v

    def put_row(r, s, v):
        for h in range(2):
            for c in range(0, tile_cols, 8):
                put(h, r, c + 8, s, v[c:min(c + 8, tile_cols), h * 128:(h + 1) * 128])

    def put_side(r, s, v, c):
        for h in range(2):
            put(h, r, c, s, v[:, h * 128:(h + 1) * 128])

    for r in range(12):
        if r >= 4:
            put_row(r, 0, grid_ref[r - 4].astype(F32))
        if r <= tile_rows - 39:
            put_row(r, 7, grid_ref[38 + r].astype(F32))

    def relay(r, _):
        for s in range(1, 7):
            put_row(r, s, grid_ref[6 * s + r - 4].astype(F32))
        return 0

    lax.fori_loop(0, 12, relay, 0)
    for h in range(2):
        for t in range(7 * SPLIT, 49):
            tap8_ref[h, t * 8:(t + 1) * 8, :] = jnp.broadcast_to(tap_ref[t // 7, t % 7:t % 7 + 1, h * 128:(h + 1) * 128].astype(F32), (8, 128))

    tap_bands(tap_ref, band_ref)

    pl.semaphore_wait(line_sem, n_lat - 1)
    for h in halos:
        h.start()

    def eight(d):
        return pl.ds(pl.multiple_of(d * 8, 8), 8)

    own = pltpu.make_async_copy(req_ref.at[eight(me)], got_ref.at[eight(me)], own_sem)
    own.start()

    def ask(k, _):
        d, to = partner(k)
        pltpu.make_async_remote_copy(
            src_ref=req_ref.at[eight(d)], dst_ref=got_ref.at[eight(me)], send_sem=req_send, recv_sem=req_recv,
            device_id=to, device_id_type=pl.DeviceIdType.MESH).start()
        return 0

    lax.fori_loop(1, devices, ask, 0)

    for h in halos:
        h.wait()
    above = jnp.where(lat > 0, 1.0, 0.0)
    below = jnp.where(lat < n_lat - 1, 1.0, 0.0)

    def block(ref, k):
        return ref[pl.ds(pl.multiple_of(k * 16, 16), 16), :].astype(F32)

    def sides(r2, s):
        k = 3 * s + r2 - 2
        a, b = block(left_ref, k), block(right_ref, k)
        for u in range(2):
            put_side(2 * r2 + u, s, a[8 * u:8 * u + 8], 0)
            put_side(2 * r2 + u, s, b[8 * u:8 * u + 8], tile_cols + 8)

    def middle(r2, _):
        for s in range(1, 7):
            sides(r2, s)
        return 0

    lax.fori_loop(0, 6, middle, 0)
    for r2 in range(2, 6):
        sides(r2, 0)
    for r2 in range(0, 4):
        sides(r2, 7)
    for r in range(4):
        put_row(r, 0, top_ref[r].astype(F32) * above)
        for n, c in ((0, 0), (1, tile_cols + 8)):
            v = corner_ref[n, (r + 1) // 2 * 16:(r + 1) // 2 * 16 + 16, :].astype(F32) * above
            put_side(r, 0, v[(r + 1) % 2 * 8:(r + 1) % 2 * 8 + 8], c)
    for r in range(7, 12):
        put_row(r, 7, bottom_ref[r - 7].astype(F32) * below)
        for n, c in ((2, 0), (3, tile_cols + 8)):
            v = corner_ref[n, (r - 7) // 2 * 16:(r - 7) // 2 * 16 + 16, :].astype(F32) * below
            put_side(r, 7, v[(r - 7) % 2 * 8:(r - 7) % 2 * 8 + 8], c)

    pack_pairs(x_ref, pack_ref)
    grid_body(x_ref, tap8_ref, pack_ref, band_ref, part_ref, mix_ref, gain_ref, up_ref, down_ref, read_ref, q_ref, first, tile_rows * n_lat)

    own.wait()
    most = pl.ds(0, (devices - 1) * 8)
    pltpu.make_async_copy(req_ref.at[most], got_ref.at[most], req_send).wait()
    pltpu.make_async_copy(req_ref.at[most], got_ref.at[most], req_recv).wait()
    cells = got_ref[pl.ds(0, devices, stride=8), :].astype(I32)
    idx_ref[...] = jnp.clip(cells, 0, tile_rows * tile_cols - 1)
    where_ref[0] = got_ref[pl.ds(1, devices, stride=8), :]
    where_ref[1] = got_ref[pl.ds(2, devices, stride=8), :]
    idx_in = pltpu.make_async_copy(idx_ref, idx_smem, idx_sem)
    idx_in.start()
    flat_weights(where_ref, w_ref)
    build_table(q_ref, table_ref, tile_rows, tile_cols)
    idx_in.wait()

    low = lax.broadcasted_iota(I32, (32, 128), 1) < 64

    share = devices // 8

    def rows(d):
        return pl.ds(pl.multiple_of(d * 64, 64), 64)

    mine = pltpu.make_async_copy(out_ref.at[rows(me)], ret_ref.at[rows(me)], own_sem)

    def send(d, to, group):
        pltpu.make_async_remote_copy(
            src_ref=out_ref.at[rows(d)], dst_ref=ret_ref.at[rows(me)], send_sem=val_send, recv_sem=val_recv.at[group],
            device_id=to, device_id_type=pl.DeviceIdType.MESH).start()

    def serve(j, _):
        those = [partner(j * unroll + u) for u in range(unroll)]
        for d, _ in those:
            read_source(idx_smem, d, table_ref, w_ref, out_ref, low)
        group = lax.div(j * unroll, share)
        pl.when(j > 0)(functools.partial(send, *those[0], group))
        pl.when(j == 0)(mine.start)
        for d, to in those[1:]:
            send(d, to, group)
        return 0

    lax.fori_loop(0, devices // unroll, serve, 0)
    wide_ref = x_ref.at[0]
    for group in range(devices // share):
        count = pl.ds(0, (share - (group == 0)) * 64)
        pltpu.make_async_copy(out_ref.at[count], ret_ref.at[count], val_recv.at[group]).wait()
        if group == 0:
            mine.wait()

        def widen(k, _):
            s = lax.rem(me + (devices - k) * turn, devices)
            wide_ref[rows(s), :] = ret_ref[rows(s), :].astype(F32)
            return 0

        lax.fori_loop(group * share, (group + 1) * share, widen, 0)

    rows_in.wait()
    most = pl.ds(0, (devices - 1) * 64)
    pltpu.make_async_copy(out_ref.at[most], ret_ref.at[most], val_send).wait()
    place_body(row_smem, half_ref, wide_ref, result_ref, x0_ref, x1_ref)


def window(owner, offsets, fractions, grid, taps, gain, up, down, read2, n_lat, n_lon):
    n = owner.shape[0] // 128
    devices = n_lat * n_lon
    tile_rows, tile_cols = grid.shape[:2]
    pairs = (tile_rows + 1) // 2
    dma = pltpu.SemaphoreType.DMA
    return pl.pallas_call(
        functools.partial(window_kernel, n_lat=n_lat, n_lon=n_lon, turn=37, unroll=8),
        out_shape=jax.ShapeDtypeStruct((64, n * 128), BF16),
        in_specs=[pl.BlockSpec(memory_space=pl.ANY if k == 3 else VM) for k in range(9)],
        out_specs=pl.BlockSpec(memory_space=VM),
        scratch_shapes=[
            VM(grid.shape, BF16), VM((128, 2048), BF16), VM((768, 2048), BF16), VM((3, 128, 128), F32), VM((devices * 8, 128), F32), VM((devices * 8, 128), F32),
            VM((pairs * 16, 256), BF16), VM((pairs * 16, 256), BF16), VM((pairs * 16, 256), BF16), VM((pairs * 16, 256), BF16),
            VM((4, tile_cols, 256), BF16), VM((5, tile_cols, 256), BF16), VM((4, 48, 256), BF16),
            VM((2, 12 * EXT * 8, 128), F32), VM((2, 49 * 8, 128), F32),
            VM((2, 2, 2, 12, PAIRS * 8 + 32, 128), BF16), VM((2, SPLIT, 1024, 256), BF16), VM((2, PAIRS * 8, 128), F32),
            VM((6, PAIRS, 2, 8, 256), F32),
            VM((6 * COLS * 8, 128), F32), VM((n, 128), I32), VM((n, 128), I32), VM((devices, 128), I32), VM((2, devices, 128), F32),
            VM((tile_rows * tile_cols, 8, 128), F32), VM((2, devices, 1024), F32), VM((devices * 64, 128), BF16),
            VM((devices * 64, 128), BF16), VM((128, 128), F32), VM((128, 128), F32),
            pltpu.SMEM((devices, 128), I32), pltpu.SMEM((n, 128), I32),
            dma((8,)), dma((8,)), dma, dma, dma, dma, dma((8,)), dma, dma, dma, pltpu.SemaphoreType.REGULAR],
        compiler_params=pltpu.CompilerParams(vmem_limit_bytes=63 << 20, has_side_effects=True, collective_id=0),
        name="window",
    )(owner.reshape(n, 128), offsets.reshape(n, 128), fractions, grid, taps, gain, up, down, read2)


def shards(grid, dw_kernel, norm_gain, w_up, w_down, w_read, owner, offsets, fractions):
    n_lat, n_lon = lax.axis_size("lat"), lax.axis_size("lon")
    return window(
        owner, offsets, fractions, grid, dw_kernel[0], norm_gain, w_up[0], w_down[0],
        w_read.T, n_lat, n_lon).T


def solution(mesh):
    return jax.shard_map(
        shards,
        mesh=mesh,
        in_specs=(P("lat", "lon", None), P(), P(), P(), P(), P(), P(("lat", "lon"), None), P(("lat", "lon")), P(None, ("lat", "lon"))),
        out_specs=P(("lat", "lon"), None),
        check_vma=False,
    )
```
